32 devices in a mesh: dp: 8 (over z, y), seq: 4 (over x, core).
Axes of the slice: x: 2, y: 2, z: 4, core: 2. Of those that a mesh axis runs over, the one named last changes fastest.
Arguments:
- queries: bfloat16 [8, 512, 2048], P('dp', 'seq'), may hold values from -6 to 6
- grad_out: bfloat16 [8, 512, 2048], P('dp', 'seq'), may hold values from -6 to 6
- encoded: bfloat16 [8, 8, 64, 896], P('dp', 'seq'), may hold values from -6 to 6
- kv_weight: bfloat16 [896, 4096], P(None, 'dp'), may hold values from -0.1875 to 0.1875
- neighbour_ids: int32 [8, 8, 2], P('dp', 'seq'), may hold values from 0 to 7, all different within a row
- slot_map: int32 [8, 8], P('dp'), may hold values from 0 to 7, each once within a row
Outputs:
- attended: bfloat16 [8, 512, 2048], P('dp', 'seq')
- grad_queries: bfloat16 [8, 512, 2048], P('dp', 'seq')
- grad_encoded: float32 [8, 8, 64, 896], P('dp', 'seq')
The draws below stay inside these ranges and needn't reach their ends.
Inputs may be any that keep to these rules, and one draw needn't show every extreme that they name: `neighbour_ids`: each span names 2 different neighbour ids of its own sequence. `slot_map`: for each sequence a permutation; storage position p lies on the seq index p // 2.
All inputs are finite; a program needn't handle non-finite values.
Results may differ from the reference program's by a relative error of at most 0.018.
Values may be sent and summed in bfloat16 or wider, within the bound.
No kernel may reach another device: no remote copies, remote signals or barrier semaphores. Data moves between devices by JAX's collectives and lax.ppermute only.
A program may use at most 64 MiB of HBM per device.

```python
import jax
import jax.numpy as jnp
from jax import lax

DE = 896
HEAD_SIZE = 128
HEADS = 16
SPAN = 64
NLEN = 64
READS = 2
HD = 2048
SPAN_DEV = 2
LENGTH = 512
SPANS = 8
NBR_GROUP = 8
SEQS = 8
N_SEQ = 4


def level_of(key, dims, split, least, largest):
    gain = 1.0
    for axis_at, blocks in split:
        draws = jax.random.uniform(jax.random.fold_in(jax.random.fold_in(key, 6), axis_at), (blocks,), jnp.float32, least / len(split), largest / len(split))
        gain = gain * jnp.repeat(jnp.exp(draws), dims[axis_at] // blocks).reshape((-1,) + (1,) * (len(dims) - 1 - axis_at))
    return gain


def different_ones(stream_key, rows, count, top, lift):
    sequence = jax.random.permutation(jax.random.fold_in(stream_key, 1), count)
    boost = sequence
    for power in range(3):
        boost = boost * boost // count
    boost = boost * lift // count
    tickets = jax.random.randint(jax.random.fold_in(stream_key, 2), (rows, count), 0, 4096) + boost
    sure = jax.random.permutation(jax.random.fold_in(stream_key, 3), rows)[jnp.arange(count) % rows]
    tickets = jnp.where(jnp.arange(rows)[:, None] == sure[None, :], 1 << 14, tickets)
    score = tickets * count + jnp.arange(count)
    return lax.top_k(score.astype(jnp.int32), top)[1].astype(jnp.int32)


def noise(stream_key, dims, scale, bound, cuts=(), held_as=jnp.bfloat16):
    result = jax.random.normal(stream_key, dims, jnp.float32) * scale
    if len(cuts) > 0:
        result = level_of(stream_key, dims, cuts, -0.22, 0.18) * result
    return jnp.clip(result, min=-bound, max=bound).astype(held_as)


def setup_inputs(seed: int = 0) -> dict:
    key_of = jax.random.split(jax.random.key(seed), 7)
    return {
        "queries": noise(key_of[0], (SEQS, LENGTH, HD), 1.0, 6.0, ((0, 8), (1, 4))),
        "grad_out": noise(key_of[1], (SEQS, LENGTH, HD), 1.0, 6.0, ((0, 8), (1, 4))),
        "encoded": noise(key_of[2], (SEQS, NBR_GROUP, NLEN, DE), 1.0, 6.0, ((0, 8), (1, 4))),
        "kv_weight": noise(key_of[3], (DE, 2 * HD), DE ** -0.5, 0.1875, ((1, 8),)),
        "neighbour_ids": different_ones(key_of[4], SEQS * SPANS, NBR_GROUP, READS, 4096).reshape((SEQS, SPANS, READS)),
        "slot_map": jax.vmap(lambda own: jax.random.permutation(own, NBR_GROUP))(jax.random.split(key_of[5], SEQS)).reshape((SEQS, NBR_GROUP)).astype(jnp.int32),
    }


def one_sequence(kv_weight, packed):
    query_rows, grad_rows, stored, chosen, slots = packed
    hidden = HEADS * HEAD_SIZE
    scale_factor = HEAD_SIZE ** -0.5
    projected = jnp.dot(stored.reshape(NBR_GROUP * NLEN, DE), kv_weight, preferred_element_type=jnp.float32)
    kv_rows = projected.astype(jnp.bfloat16).reshape(NBR_GROUP, NLEN, 2 * hidden)
    matches = chosen[:, :, None] == jnp.arange(NBR_GROUP, dtype=jnp.int32)[None, None, :]
    positions = jnp.sum(jnp.where(matches, slots[None, None, :], 0), axis=2).astype(jnp.int32)
    flat_pos = positions.reshape(SPANS * READS)
    kv_reads = jnp.take(kv_rows, flat_pos, axis=0).reshape(SPANS, READS * NLEN, 2 * hidden)
    keys = kv_reads[:, :, :hidden].reshape(SPANS, READS * NLEN, HEADS, HEAD_SIZE).astype(jnp.float32)
    values = kv_reads[:, :, hidden:].reshape(SPANS, READS * NLEN, HEADS, HEAD_SIZE).astype(jnp.float32)
    query_tiles = query_rows.reshape(SPANS, SPAN, HEADS, HEAD_SIZE).astype(jnp.float32)
    grad_tiles = grad_rows.reshape(SPANS, SPAN, HEADS, HEAD_SIZE).astype(jnp.float32)
    scores = jnp.einsum('cqhd,ckhd->chqk', query_tiles, keys) * scale_factor
    expos = jnp.exp(scores)
    probs = expos / jnp.sum(expos, axis=-1, keepdims=True)
    probs_low = probs.astype(jnp.bfloat16).astype(jnp.float32)
    attended = jnp.einsum('chqk,ckhd->cqhd', probs_low, values).astype(jnp.bfloat16).reshape(LENGTH, hidden)
    d_probs = jnp.einsum('cqhd,ckhd->chqk', grad_tiles, values)
    delta = jnp.sum(probs * d_probs, axis=-1, keepdims=True)
    d_scores = (probs * (d_probs - delta) * scale_factor).astype(jnp.bfloat16).astype(jnp.float32)
    grad_queries = jnp.einsum('chqk,ckhd->cqhd', d_scores, keys).astype(jnp.bfloat16).reshape(LENGTH, hidden)
    d_keys = jnp.einsum('chqk,cqhd->ckhd', d_scores, query_tiles).reshape(SPANS * READS, NLEN, hidden)
    d_values = jnp.einsum('chqk,cqhd->ckhd', probs_low, grad_tiles).reshape(SPANS * READS, NLEN, hidden)
    grad_reads = jnp.concatenate([d_keys, d_values], axis=-1).astype(jnp.bfloat16)
    enc_reads = jnp.dot(grad_reads.reshape(SPANS * READS * NLEN, 2 * hidden), kv_weight.T, preferred_element_type=jnp.float32)
    grad_blocks = enc_reads.reshape(N_SEQ, SPAN_DEV * READS, NLEN, DE)
    pos_blocks = flat_pos.reshape(N_SEQ, SPAN_DEV * READS)
    onehot = (pos_blocks[:, :, None] == jnp.arange(NBR_GROUP, dtype=jnp.int32)[None, None, :]).astype(jnp.float32)
    partial_value = jnp.einsum('brn,brlk->bnlk', onehot, grad_blocks, precision=lax.Precision.HIGHEST)
    rounded = lax.optimization_barrier(partial_value.astype(jnp.bfloat16))
    grad_encoded = jnp.sum(rounded.astype(jnp.float32), axis=0)
    return attended, grad_queries, grad_encoded


def reference(queries, grad_out, encoded, kv_weight, neighbour_ids, slot_map):
    return lax.map(lambda packed: one_sequence(kv_weight, packed), (queries, grad_out, encoded, neighbour_ids, slot_map))
```

```python
import functools

import jax
import jax.numpy as jnp
from jax import lax
from jax.experimental import pallas as pl
from jax.experimental.pallas import tpu as pltpu
from jax.sharding import PartitionSpec as P

HEAD_SIZE = 128
HEADS = 16
SPAN = 64
NLEN = 64
READS = 2
VMEM_BYTES = 48 * 1024 * 1024

NT = (((1,), (1,)), ((), ()))
TN = (((0,), (0,)), ((), ()))


def xor_send(value, axis, size, bit):
    return lax.ppermute(value, axis, [(i, i ^ bit) for i in range(size)])


def bit_reverse(index, bits):
    result = index * 0
    for i in range(bits):
        result = result + (((index >> i) & 1) << (bits - 1 - i))
    return result


def pack_body(seq_size, meta, queries, grad_out, *pieces):
    own, first = meta[0], meta[1]
    for k in range(seq_size):
        for r in range(HEADS // seq_size):
            column = pl.multiple_of(((first ^ r) * seq_size + (own ^ k)) * HEAD_SIZE, HEAD_SIZE)
            place = slice(r * HEAD_SIZE, (r + 1) * HEAD_SIZE)
            pieces[k][0, :, place] = queries[0, :, pl.ds(column, HEAD_SIZE)]
            pieces[k][1, :, place] = grad_out[0, :, pl.ds(column, HEAD_SIZE)]


def pack(meta, queries, grad_out, seq_size):
    tokens = queries.shape[1]
    shape = jax.ShapeDtypeStruct((2, tokens, HEADS // seq_size * HEAD_SIZE), jnp.bfloat16)
    return pl.pallas_call(
        functools.partial(pack_body, seq_size),
        out_shape=[shape] * seq_size,
        in_specs=[pl.BlockSpec(memory_space=pltpu.SMEM)] + [pl.BlockSpec(memory_space=pltpu.VMEM)] * 2,
        out_specs=[pl.BlockSpec(memory_space=pltpu.VMEM)] * seq_size,
        compiler_params=pltpu.CompilerParams(vmem_limit_bytes=VMEM_BYTES),
        name="pack",
    )(meta, queries, grad_out)


def attention_body(seq_size, spans, heads, has_prior, *refs):
    meta = refs[0]
    count = len(heads)
    enc_low, enc_high = refs[1], refs[2]
    weights = refs[3 : 3 + 2 * count]
    at = 3 + 2 * count
    pieces = refs[at : at + seq_size]
    at += seq_size
    prior = refs[at] if has_prior else None
    at += has_prior
    outs = refs[at : at + seq_size]
    grad_rows = refs[at + seq_size]
    pair, kv, d_kv = refs[at + seq_size + 1 :]
    half = enc_low.shape[0]
    bits = seq_size.bit_length() - 1
    scale = HEAD_SIZE ** (-0.5)
    keys_first = meta[2] == 1
    for i, head in enumerate(heads):
        first, second = weights[2 * i][...], weights[2 * i + 1][...]
        pair[:, :HEAD_SIZE] = jnp.where(keys_first, first, second)
        pair[:, HEAD_SIZE:] = jnp.where(keys_first, second, first)
        kv[:half] = jnp.dot(enc_low[...], pair[...], preferred_element_type=jnp.float32).astype(jnp.bfloat16)
        kv[half:] = jnp.dot(enc_high[...], pair[...], preferred_element_type=jnp.float32).astype(jnp.bfloat16)
        d_kv[...] = jnp.zeros_like(d_kv)
        columns = slice(head * HEAD_SIZE, (head + 1) * HEAD_SIZE)
        out_columns = slice(i * HEAD_SIZE, (i + 1) * HEAD_SIZE)
        for k in range(seq_size):
            order = bit_reverse(k, bits)
            for c in range(spans):
                rows = slice(c * SPAN, (c + 1) * SPAN)
                starts = [
                    pl.multiple_of(meta[4 + (order * spans + c) * READS + r] * NLEN, NLEN)
                    for r in range(READS)
                ]
                read = jnp.concatenate([kv[pl.ds(start, NLEN), :] for start in starts], axis=0)
                keys, values = read[:, :HEAD_SIZE], read[:, HEAD_SIZE:]
                query = pieces[k][0, rows, columns]
                grad = pieces[k][1, rows, columns]
                scores = lax.dot_general(query, keys, NT, preferred_element_type=jnp.float32) * scale
                d_probs = lax.dot_general(grad, values, NT, preferred_element_type=jnp.float32)
                expos = jnp.exp(scores)
                probs = expos / jnp.sum(expos, axis=-1, keepdims=True)
                probs_low = probs.astype(jnp.bfloat16)
                delta = jnp.sum(probs * d_probs, axis=-1, keepdims=True)
                d_scores = (probs * (d_probs - delta) * scale).astype(jnp.bfloat16)
                outs[k][0, rows, out_columns] = jnp.dot(
                    probs_low, values, preferred_element_type=jnp.float32
                ).astype(jnp.bfloat16)
                outs[k][1, rows, out_columns] = jnp.dot(
                    d_scores, keys, preferred_element_type=jnp.float32
                ).astype(jnp.bfloat16)
                d_keys = lax.dot_general(d_scores, query, TN, preferred_element_type=jnp.float32)
                d_values = lax.dot_general(probs_low, grad, TN, preferred_element_type=jnp.float32)
                for r, start in enumerate(starts):
                    part = slice(r * NLEN, (r + 1) * NLEN)
                    d_kv[pl.ds(start, NLEN), :HEAD_SIZE] += d_keys[part]
                    d_kv[pl.ds(start, NLEN), HEAD_SIZE:] += d_values[part]
        term = lax.dot_general(
            d_kv[...].astype(jnp.bfloat16), pair[...], NT, preferred_element_type=jnp.float32
        )
        if i == 0:
            grad_rows[...] = term + prior[...] if has_prior else term
        else:
            grad_rows[...] += term


def attention(meta, enc_low, enc_high, weights, pieces, heads, spans, prior):
    seq_size = len(pieces)
    tokens = pieces[0].shape[1]
    rows = 2 * enc_low.shape[0]
    width = enc_low.shape[1]
    count = len(heads)
    prior = [] if prior is None else [prior]
    vmem = pl.BlockSpec(memory_space=pltpu.VMEM)
    operands = [enc_low, enc_high, *weights, *pieces, *prior]
    out_shape = [jax.ShapeDtypeStruct((2, tokens, count * HEAD_SIZE), jnp.bfloat16)] * seq_size
    out_shape.append(jax.ShapeDtypeStruct((rows, width), jnp.float32))
    outs = pl.pallas_call(
        functools.partial(attention_body, seq_size, spans, heads, len(prior)),
        out_shape=out_shape,
        in_specs=[pl.BlockSpec(memory_space=pltpu.SMEM)] + [vmem] * len(operands),
        out_specs=[vmem] * len(out_shape),
        scratch_shapes=[
            pltpu.VMEM((width, 2 * HEAD_SIZE), jnp.bfloat16),
            pltpu.VMEM((rows, 2 * HEAD_SIZE), jnp.bfloat16),
            pltpu.VMEM((rows, 2 * HEAD_SIZE), jnp.float32),
        ],
        compiler_params=pltpu.CompilerParams(vmem_limit_bytes=VMEM_BYTES),
        cost_estimate=pl.CostEstimate(
            flops=count * (8 * rows * width * HEAD_SIZE), bytes_accessed=2 * rows * width, transcendentals=0
        ),
        name="attention",
    )(meta, *operands)
    return outs[:-1], outs[-1]


def unpack_body(seq_size, groups, meta, *refs):
    count = len(groups) * seq_size
    attended, grad_queries, sems = refs[count:]
    own, first = meta[0], meta[1]
    copies = []
    for g, heads in enumerate(groups):
        for k in range(seq_size):
            for i, r in enumerate(heads):
                column = pl.multiple_of(((first ^ r) * seq_size + (own ^ k)) * HEAD_SIZE, HEAD_SIZE)
                for which, target in enumerate((attended, grad_queries)):
                    copy = pltpu.make_async_copy(
                        refs[g * seq_size + k].at[which, :, pl.ds(i * HEAD_SIZE, HEAD_SIZE)],
                        target.at[0, :, pl.ds(column, HEAD_SIZE)],
                        sems.at[len(copies)],
                    )
                    copy.start()
                    copies.append(copy)
    for copy in copies:
        copy.wait()


def unpack(meta, parts, groups, seq_size):
    tokens = parts[0].shape[1]
    shape = jax.ShapeDtypeStruct((1, tokens, HEADS * HEAD_SIZE), jnp.bfloat16)
    anywhere = pl.BlockSpec(memory_space=pl.ANY)
    return pl.pallas_call(
        functools.partial(unpack_body, seq_size, groups),
        out_shape=[shape, shape],
        in_specs=[pl.BlockSpec(memory_space=pltpu.SMEM)] + [anywhere] * len(parts),
        out_specs=[anywhere, anywhere],
        scratch_shapes=[pltpu.SemaphoreType.DMA((2 * HEADS,))],
        name="unpack",
    )(meta, *parts)


def gather_weights(kv_weight, own, dp_size, seq_size):
    blocks = 2 * HEADS // dp_size
    if dp_size == 8 and blocks == seq_size:
        mine = lax.dynamic_slice_in_dim(kv_weight, own * HEAD_SIZE, HEAD_SIZE, axis=1)
        send = functools.partial(xor_send, axis="dp", size=dp_size)
        far = send(mine, bit=4)
        near = send(mine, bit=2)
        side = send(mine, bit=1)
        side_far = send(far, bit=1)
        near_far = send(far, bit=2)
        side_near = send(side, bit=2)
        side_near_far = send(near_far, bit=1)
        return [(mine, far), (side, side_far), (near, near_far), (side_near, side_near_far)]
    whole = lax.all_gather(kv_weight, "dp", axis=1, tiled=True)
    pairs = []
    for r in range(HEADS // seq_size):
        column = (r * seq_size + own) * HEAD_SIZE
        pairs.append(
            tuple(
                lax.dynamic_slice_in_dim(whole, column + part * HEADS * HEAD_SIZE, HEAD_SIZE, axis=1)
                for part in range(2)
            )
        )
    return pairs


def per_device(dp_size, seq_size, queries, grad_out, encoded, kv_weight, neighbour_ids, slot_map):
    own = lax.axis_index("seq")
    place = lax.axis_index("dp")
    bits = seq_size.bit_length() - 1
    stored = encoded.shape[1]
    spans = neighbour_ids.shape[1]
    width = encoded.shape[3]
    split = dp_size == 8 and 2 * HEADS == dp_size * seq_size
    first = place % (HEADS // seq_size) if split else place * 0
    keys_first = (place < dp_size // 2).astype(jnp.int32) if split else place * 0 + 1
    send = functools.partial(xor_send, axis="seq", size=seq_size)

    pool_size = slot_map.shape[1]
    matches = neighbour_ids[0][:, :, None] == jnp.arange(pool_size, dtype=jnp.int32)[None, None, :]
    positions = jnp.sum(jnp.where(matches, slot_map[0][None, None, :], 0), axis=2).reshape(-1)
    rows = encoded[0].reshape(stored * NLEN, width)
    head_meta = jnp.stack([own, first, keys_first, place])
    pieces = pack(head_meta, queries, grad_out, seq_size)
    pieces = [pieces[0]] + [send(pieces[k], bit=k) for k in range(1, seq_size)]
    for level in range(bits - 1, 0, -1):
        rows = jnp.concatenate([rows, send(rows, bit=1 << level)], axis=0)
    enc_low, enc_high = rows, send(rows, bit=1)
    for level in range(bits - 1, -1, -1):
        positions = jnp.concatenate([positions, send(positions, bit=1 << level)])
    relative = bit_reverse((positions // stored) ^ own, bits) * stored + positions % stored
    meta = jnp.concatenate([head_meta, relative])

    pairs = gather_weights(kv_weight, own, dp_size, seq_size)
    groups = [(0, 1), (2, 3)] if len(pairs) == 4 else [tuple(range(len(pairs)))]
    parts = []
    grads = None
    for heads in groups:
        weights = [block for head in heads for block in pairs[head]]
        outs, grads = attention(meta, enc_low, enc_high, weights, pieces, heads, spans, grads)
        parts.append([outs[0]] + [send(outs[k], bit=k) for k in range(1, seq_size)])
    for level in range(bits):
        half = grads.shape[0] // 2
        arrived = send(grads[half:].astype(jnp.bfloat16), bit=1 << level)
        grads = grads[:half] + arrived.astype(jnp.float32)
    flat = [part for group in parts for part in group]
    attended, grad_queries = unpack(head_meta, flat, groups, seq_size)
    return attended, grad_queries, grads.reshape(1, stored, NLEN, width)


def solution(mesh):
    in_specs = (
        P("dp", "seq", None),
        P("dp", "seq", None),
        P("dp", "seq", None, None),
        P(None, "dp"),
        P("dp", "seq", None),
        P("dp", None),
    )
    out_specs = (P("dp", "seq", None), P("dp", "seq", None), P("dp", "seq", None, None))
    return jax.shard_map(
        functools.partial(per_device, mesh.shape["dp"], mesh.shape["seq"]),
        mesh=mesh,
        in_specs=in_specs,
        out_specs=out_specs,
        check_vma=False,
    )
```

```python
import functools

import jax
import jax.numpy as jnp
from jax import lax
from jax.experimental import pallas as pl
from jax.experimental.pallas import tpu as pltpu
from jax.sharding import PartitionSpec as P

HEAD_SIZE = 128
HEADS = 16
SPAN = 64
NLEN = 64
READS = 2

NT = (((1,), (1,)), ((), ()))
TN = (((0,), (0,)), ((), ()))
EXTRA = 16


def vmem_bytes(rows):
    return (8 << 20) + rows * (16 << 10)


def xor_send(value, axis, size, bit):
    return lax.ppermute(value, axis, [(i, i ^ bit) for i in range(size)])


def bit_reverse(index, bits):
    result = index * 0
    for i in range(bits):
        result = result + (((index >> i) & 1) << (bits - 1 - i))
    return result


def pack_body(seq_size, reads, meta, queries, grad_out, *pieces):
    own, first = meta[0], meta[1]
    tokens = queries.shape[1]
    lanes = lax.broadcasted_iota(jnp.int32, (EXTRA, pieces[0].shape[1]), 1)
    positions = jnp.zeros(lanes.shape, jnp.int32)
    for i in range(reads):
        positions = jnp.where(lanes == i, meta[4 + i], positions)
    positions = positions.astype(jnp.float32).astype(jnp.bfloat16)
    for k in range(seq_size):
        for r in range(HEADS // seq_size):
            column = pl.multiple_of(((first ^ r) * seq_size + (own ^ k)) * HEAD_SIZE, HEAD_SIZE)
            place = slice(r * HEAD_SIZE, (r + 1) * HEAD_SIZE)
            pieces[k][:tokens, place] = queries[0, :, pl.ds(column, HEAD_SIZE)]
            pieces[k][tokens : 2 * tokens, place] = grad_out[0, :, pl.ds(column, HEAD_SIZE)]
        pieces[k][2 * tokens :, :] = positions


def pack(meta, queries, grad_out, seq_size):
    tokens = queries.shape[1]
    shape = jax.ShapeDtypeStruct((2 * tokens + EXTRA, HEADS // seq_size * HEAD_SIZE), jnp.bfloat16)
    return pl.pallas_call(
        functools.partial(pack_body, seq_size, meta.shape[0] - 4),
        out_shape=[shape] * seq_size,
        in_specs=[pl.BlockSpec(memory_space=pltpu.SMEM)] + [pl.BlockSpec(memory_space=pltpu.VMEM)] * 2,
        out_specs=[pl.BlockSpec(memory_space=pltpu.VMEM)] * seq_size,
        compiler_params=pltpu.CompilerParams(vmem_limit_bytes=vmem_bytes(0)),
        name="pack",
    )(meta, queries, grad_out)


def attention_body(seq_size, spans, heads, has_prior, last, *refs):
    count = len(heads)
    meta, refs = refs[0], refs[1:]
    stored, refs = refs[:seq_size], refs[seq_size:]
    weights, refs = refs[: 2 * count], refs[2 * count :]
    pieces, refs = refs[:seq_size], refs[seq_size:]
    prior, refs = (refs[0], refs[1:]) if has_prior else (None, refs)
    outs, refs = refs[:seq_size], refs[seq_size:]
    grads, refs = (refs[:2], refs[2:]) if last else (refs[:1], refs[1:])
    enc, pair, kv, d_kv = refs
    block = stored[0].shape[0]
    rows = enc.shape[0]
    tokens = spans * SPAN
    scale = HEAD_SIZE ** (-0.5)
    keys_first = meta[2] == 1
    for i in range(seq_size):
        enc[i * block : (i + 1) * block] = stored[i][...]
    spots = []
    for k in range(seq_size):
        for c in range(spans):
            at = 4 + (k * spans + c) * READS
            spots.append((k, c, [pl.multiple_of(meta[at + r] * NLEN, NLEN) for r in range(READS)]))
    for i, head in enumerate(heads):
        first, second = weights[2 * i][...], weights[2 * i + 1][...]
        wide = slice(2 * i * HEAD_SIZE, 2 * (i + 1) * HEAD_SIZE)
        pair[:, 2 * i * HEAD_SIZE : (2 * i + 1) * HEAD_SIZE] = jnp.where(keys_first, first, second)
        pair[:, (2 * i + 1) * HEAD_SIZE : (2 * i + 2) * HEAD_SIZE] = jnp.where(keys_first, second, first)
        kv[...] = jnp.dot(enc[...], pair[:, wide], preferred_element_type=jnp.float32).astype(jnp.bfloat16)
        d_kv[:, wide] = jnp.zeros((rows, 2 * HEAD_SIZE), jnp.float32)
        columns = slice(head * HEAD_SIZE, (head + 1) * HEAD_SIZE)
        out_columns = slice(i * HEAD_SIZE, (i + 1) * HEAD_SIZE)
        reads, queries, grad_rows, scores, d_probs = [], [], [], [], []
        for k, c, starts in spots:
            read = jnp.concatenate([kv[pl.ds(start, NLEN), :] for start in starts], axis=0)
            query = pieces[k][c * SPAN : (c + 1) * SPAN, columns]
            grad = pieces[k][tokens + c * SPAN : tokens + (c + 1) * SPAN, columns]
            reads.append((read[:, :HEAD_SIZE], read[:, HEAD_SIZE:]))
            queries.append(query)
            grad_rows.append(grad)
            scores.append(lax.dot_general(query, reads[-1][0], NT, preferred_element_type=jnp.float32))
            d_probs.append(lax.dot_general(grad, reads[-1][1], NT, preferred_element_type=jnp.float32))
        probs_low, d_scores = [], []
        for score, d_prob in zip(scores, d_probs):
            expos = jnp.exp(score * scale)
            probs = expos / jnp.sum(expos, axis=-1, keepdims=True)
            delta = jnp.sum(probs * d_prob, axis=-1, keepdims=True)
            probs_low.append(probs.astype(jnp.bfloat16))
            d_scores.append((probs * (d_prob - delta) * scale).astype(jnp.bfloat16))
        for n, (k, c, starts) in enumerate(spots):
            keys, values = reads[n]
            span = slice(c * SPAN, (c + 1) * SPAN)
            outs[k][0, span, out_columns] = jnp.dot(
                probs_low[n], values, preferred_element_type=jnp.float32
            ).astype(jnp.bfloat16)
            outs[k][1, span, out_columns] = jnp.dot(
                d_scores[n], keys, preferred_element_type=jnp.float32
            ).astype(jnp.bfloat16)
            d_keys = lax.dot_general(d_scores[n], queries[n], TN, preferred_element_type=jnp.float32)
            d_values = lax.dot_general(probs_low[n], grad_rows[n], TN, preferred_element_type=jnp.float32)
            both = jnp.concatenate([d_keys, d_values], axis=1)
            for r, start in enumerate(starts):
                d_kv[pl.ds(start, NLEN), wide] += both[r * NLEN : (r + 1) * NLEN]
    half = rows // 2
    for part in range(2):
        place = slice(part * half, (part + 1) * half)
        term = lax.dot_general(
            d_kv[place, :].astype(jnp.bfloat16), pair[...], NT, preferred_element_type=jnp.float32
        )
        if has_prior:
            term = term + prior[place, :].astype(jnp.float32)
        if last:
            grads[part][...] = term.astype(grads[part].dtype)
        else:
            grads[0][place, :] = term.astype(grads[0].dtype)


def attention(meta, stored, weights, pieces, heads, spans, prior, last):
    seq_size = len(pieces)
    block, width = stored[0].shape
    rows = seq_size * block
    count = len(heads)
    prior = [] if prior is None else [prior]
    vmem = pl.BlockSpec(memory_space=pltpu.VMEM)
    operands = [*stored, *weights, *pieces, *prior]
    out_shape = [jax.ShapeDtypeStruct((2, spans * SPAN, count * HEAD_SIZE), jnp.bfloat16)] * seq_size
    if last:
        out_shape.append(jax.ShapeDtypeStruct((rows // 2, width), jnp.float32))
        out_shape.append(jax.ShapeDtypeStruct((rows // 2, width), jnp.bfloat16))
    else:
        out_shape.append(jax.ShapeDtypeStruct((rows, width), jnp.bfloat16))
    outs = pl.pallas_call(
        functools.partial(attention_body, seq_size, spans, heads, len(prior), last),
        out_shape=out_shape,
        in_specs=[pl.BlockSpec(memory_space=pltpu.SMEM)] + [vmem] * len(operands),
        out_specs=[vmem] * len(out_shape),
        scratch_shapes=[
            pltpu.VMEM((rows, width), jnp.bfloat16),
            pltpu.VMEM((width, 2 * count * HEAD_SIZE), jnp.bfloat16),
            pltpu.VMEM((rows, 2 * HEAD_SIZE), jnp.bfloat16),
            pltpu.VMEM((rows, 2 * count * HEAD_SIZE), jnp.float32),
        ],
        compiler_params=pltpu.CompilerParams(vmem_limit_bytes=vmem_bytes(rows)),
        cost_estimate=pl.CostEstimate(
            flops=count * 32 * rows * width * HEAD_SIZE, bytes_accessed=4 * rows * width, transcendentals=0
        ),
        name="attention",
    )(meta, *operands)
    return outs[:seq_size], outs[seq_size:]


def unpack_body(seq_size, groups, meta, *refs):
    count = len(groups) * seq_size
    attended, grad_queries = refs[count:]
    own, first = meta[0], meta[1]
    for g, heads in enumerate(groups):
        for k in range(seq_size):
            for i, r in enumerate(heads):
                column = pl.multiple_of(((first ^ r) * seq_size + (own ^ k)) * HEAD_SIZE, HEAD_SIZE)
                place = slice(i * HEAD_SIZE, (i + 1) * HEAD_SIZE)
                attended[0, :, pl.ds(column, HEAD_SIZE)] = refs[g * seq_size + k][0, :, place]
                grad_queries[0, :, pl.ds(column, HEAD_SIZE)] = refs[g * seq_size + k][1, :, place]


def unpack(meta, parts, groups, seq_size):
    tokens = parts[0].shape[1]
    shape = jax.ShapeDtypeStruct((1, tokens, HEADS * HEAD_SIZE), jnp.bfloat16)
    vmem = pl.BlockSpec(memory_space=pltpu.VMEM)
    return pl.pallas_call(
        functools.partial(unpack_body, seq_size, groups),
        out_shape=[shape, shape],
        in_specs=[pl.BlockSpec(memory_space=pltpu.SMEM)] + [vmem] * len(parts),
        out_specs=[vmem, vmem],
        compiler_params=pltpu.CompilerParams(vmem_limit_bytes=vmem_bytes(0)),
        name="unpack",
    )(meta, *parts)


def weight_slice(kv_weight, column):
    return lax.dynamic_slice_in_dim(kv_weight, column, HEAD_SIZE, axis=1)


def gather_split(mine, dp_size):
    send = functools.partial(xor_send, axis="dp", size=dp_size)
    far = send(mine, bit=4)
    near = send(mine, bit=2)
    side = send(mine, bit=1)
    near_far = send(far, bit=2)
    side_far = send(far, bit=1)
    side_near = send(side, bit=2)
    side_near_far = send(near_far, bit=1)
    return [(mine, far), (side, side_far), (near, near_far), (side_near, side_near_far)]


def gather_whole(kv_weight, own, seq_size):
    whole = lax.all_gather(kv_weight, "dp", axis=1, tiled=True)
    pairs = []
    for r in range(HEADS // seq_size):
        column = (r * seq_size + own) * HEAD_SIZE
        pairs.append((weight_slice(whole, column), weight_slice(whole, column + HEADS * HEAD_SIZE)))
    return pairs


def per_device(dp_size, seq_size, queries, grad_out, encoded, kv_weight, neighbour_ids, slot_map):
    own = lax.axis_index("seq")
    place = lax.axis_index("dp")
    bits = seq_size.bit_length() - 1
    per_owner = encoded.shape[1]
    spans = neighbour_ids.shape[1]
    tokens = queries.shape[1]
    width = encoded.shape[3]
    pool_size = slot_map.shape[1]
    assert pool_size <= 256 and 1 << bits == seq_size
    split = dp_size == 8 and 2 * HEADS == dp_size * seq_size
    send = functools.partial(xor_send, axis="seq", size=seq_size)

    if split:
        mine = weight_slice(kv_weight, own * HEAD_SIZE)
        mine, queries, grad_out, encoded, neighbour_ids = lax.optimization_barrier(
            (mine, queries, grad_out, encoded, neighbour_ids)
        )
        pairs = gather_split(mine, dp_size)
        first = place % (HEADS // seq_size)
        keys_first = (place < dp_size // 2).astype(jnp.int32)
        groups = [(0,), (1, 2), (3,)]
    else:
        pairs = gather_whole(kv_weight, own, seq_size)
        first, keys_first = place * 0, place * 0 + 1
        groups = [tuple(range(HEADS // seq_size))]

    matches = neighbour_ids[0][:, :, None] == jnp.arange(pool_size, dtype=jnp.int32)[None, None, :]
    positions = jnp.sum(jnp.where(matches, slot_map[0][None, None, :], 0), axis=2).reshape(-1)
    head_meta = jnp.stack([own, first, keys_first, place])
    pieces = pack(jnp.concatenate([head_meta, positions]), queries, grad_out, seq_size)
    pieces = [pieces[0]] + [send(pieces[k], bit=k) for k in range(1, seq_size)]
    stored = [encoded[0].reshape(per_owner * NLEN, width)]
    for level in range(bits - 1, -1, -1):
        stored = stored + [send(rows, bit=1 << level) for rows in stored]
    positions = jnp.concatenate(
        [positions]
        + [piece[2 * tokens, : spans * READS].astype(jnp.int32) for piece in pieces[1:]]
    )
    relative = bit_reverse((positions // per_owner) ^ own, bits) * per_owner + positions % per_owner
    meta = jnp.concatenate([head_meta, relative])

    parts, grads = [], [None]
    for heads in groups:
        weights = [block for head in heads for block in pairs[head]]
        outs, grads = attention(
            meta, stored, weights, pieces, heads, spans, grads[0], heads == groups[-1]
        )
        parts = parts + [outs[0]] + [send(outs[k], bit=k) for k in range(1, seq_size)]
    total, leaving = grads
    for level in range(bits):
        total = total + send(leaving, bit=1 << level).astype(jnp.float32)
        half = total.shape[0] // 2
        if level < bits - 1:
            total, leaving = total[:half], total[half:].astype(jnp.bfloat16)
    attended, grad_queries = unpack(head_meta, parts, groups, seq_size)
    return attended, grad_queries, total.reshape(1, per_owner, NLEN, width)


def solution(mesh):
    in_specs = (
        P("dp", "seq", None),
        P("dp", "seq", None),
        P("dp", "seq", None, None),
        P(None, "dp"),
        P("dp", "seq", None),
        P("dp", None),
    )
    out_specs = (P("dp", "seq", None), P("dp", "seq", None), P("dp", "seq", None, None))
    return jax.shard_map(
        functools.partial(per_device, mesh.shape["dp"], mesh.shape["seq"]),
        mesh=mesh,
        in_specs=in_specs,
        out_specs=out_specs,
        check_vma=False,
    )
```

```python
import functools

import jax
import jax.numpy as jnp
from jax import lax
from jax.experimental import pallas as pl
from jax.experimental.pallas import tpu as pltpu
from jax.sharding import PartitionSpec as P

HEAD_SIZE = 128
HEADS = 16
SPAN = 64
NLEN = 64
READS = 2

NT = (((1,), (1,)), ((), ()))
TN = (((0,), (0,)), ((), ()))
EXTRA = 16


def vmem_bytes(rows):
    return (8 << 20) + rows * (16 << 10)


def xor_send(value, axis, size, bit):
    return lax.ppermute(value, axis, [(i, i ^ bit) for i in range(size)])


def bit_reverse(index, bits):
    result = index * 0
    for i in range(bits):
        result = result + (((index >> i) & 1) << (bits - 1 - i))
    return result


def bundles(seq_size, item, dtype):
    sizes = [1] + [1 << b for b in range(seq_size.bit_length() - 1)]
    return [jax.ShapeDtypeStruct((size, *item), dtype) for size in sizes]


def item_of(refs, k):
    return refs[k.bit_length()].at[k - ((1 << k.bit_length()) >> 1)]


def exchange(arrays, seq_size):
    waiting = {b: [(0, array)] for b, array in enumerate(arrays[1:])}
    found = {0: arrays[0][0]}
    for b in reversed(range(len(arrays) - 1)):
        for origin, array in waiting[b]:
            arrived = xor_send(array, "seq", seq_size, 1 << b)
            origin = origin | (1 << b)
            found[origin] = arrived[0]
            for c in range(b):
                waiting[c].append((origin, arrived[1 << c : 2 << c]))
    return [found[j] for j in range(seq_size)]


def pack_body(seq_size, reads, groups, meta, queries, grad_out, *refs):
    own, first = meta[0], meta[1]
    tokens = queries.shape[1]
    each = len(refs) // len(groups)
    for g, heads in enumerate(groups):
        arrays = refs[g * each : (g + 1) * each]
        for k in range(seq_size):
            piece = item_of(arrays, k)
            for i, r in enumerate(heads):
                column = pl.multiple_of(((first ^ r) * seq_size + (own ^ k)) * HEAD_SIZE, HEAD_SIZE)
                place = slice(i * HEAD_SIZE, (i + 1) * HEAD_SIZE)
                piece[:tokens, place] = queries[0, :, pl.ds(column, HEAD_SIZE)]
                piece[tokens : 2 * tokens, place] = grad_out[0, :, pl.ds(column, HEAD_SIZE)]
    lanes = lax.broadcasted_iota(jnp.int32, (EXTRA, refs[0].shape[2]), 1)
    positions = jnp.zeros(lanes.shape, jnp.int32)
    for i in range(reads):
        positions = jnp.where(lanes == i, meta[4 + i], positions)
    positions = positions.astype(jnp.float32).astype(jnp.bfloat16)
    for k in range(seq_size):
        item_of(refs[:each], k)[2 * tokens :, :] = positions


def pack(meta, queries, grad_out, groups, seq_size):
    tokens = queries.shape[1]
    vmem = pl.BlockSpec(memory_space=pltpu.VMEM)
    out_shape = []
    for g, heads in enumerate(groups):
        rows = 2 * tokens + (EXTRA if g == 0 else 0)
        out_shape += bundles(seq_size, (rows, len(heads) * HEAD_SIZE), jnp.bfloat16)
    outs = pl.pallas_call(
        functools.partial(pack_body, seq_size, meta.shape[0] - 4, groups),
        out_shape=out_shape,
        in_specs=[pl.BlockSpec(memory_space=pltpu.SMEM)] + [vmem] * 2,
        out_specs=[vmem] * len(out_shape),
        compiler_params=pltpu.CompilerParams(vmem_limit_bytes=vmem_bytes(0)),
        name="pack",
    )(meta, queries, grad_out)
    each = len(outs) // len(groups)
    return [outs[g * each : (g + 1) * each] for g in range(len(groups))]


def attention_body(seq_size, spans, takes, has_prior, last, *refs):
    count = len(takes)
    sources = max(source for source, _ in takes) + 1
    meta, refs = refs[0], refs[1:]
    stored, refs = refs[:seq_size], refs[seq_size:]
    weights, refs = refs[: 2 * count], refs[2 * count :]
    pieces, refs = refs[: sources * seq_size], refs[sources * seq_size :]
    prior, refs = (refs[0], refs[1:]) if has_prior else (None, refs)
    levels = seq_size.bit_length()
    outs, refs = refs[:levels], refs[levels:]
    grads, refs = (refs[:2], refs[2:]) if last else (refs[:1], refs[1:])
    enc, pair, kv, d_kv = refs
    block = stored[0].shape[0]
    rows = enc.shape[0]
    tokens = spans * SPAN
    scale = HEAD_SIZE ** (-0.5)
    keys_first = meta[2] == 1
    for i in range(seq_size):
        enc[i * block : (i + 1) * block] = stored[i][...]
    spots = []
    for k in range(seq_size):
        for c in range(spans):
            at = 4 + (k * spans + c) * READS
            spots.append((k, c, [pl.multiple_of(meta[at + r] * NLEN, NLEN) for r in range(READS)]))
    for i in range(count):
        first, second = weights[2 * i][...], weights[2 * i + 1][...]
        wide = slice(2 * i * HEAD_SIZE, 2 * (i + 1) * HEAD_SIZE)
        pair[:, 2 * i * HEAD_SIZE : (2 * i + 1) * HEAD_SIZE] = jnp.where(keys_first, first, second)
        pair[:, (2 * i + 1) * HEAD_SIZE : (2 * i + 2) * HEAD_SIZE] = jnp.where(keys_first, second, first)
        kv[...] = jnp.dot(enc[...], pair[:, wide], preferred_element_type=jnp.float32).astype(jnp.bfloat16)
        d_kv[:, wide] = jnp.zeros((rows, 2 * HEAD_SIZE), jnp.float32)
        columns = slice(i * HEAD_SIZE, (i + 1) * HEAD_SIZE)
        source, at = takes[i]
        taken = slice(at * HEAD_SIZE, (at + 1) * HEAD_SIZE)
        reads, queries, grad_rows, scores, d_probs = [], [], [], [], []
        for k, c, starts in spots:
            read = jnp.concatenate([kv[pl.ds(start, NLEN), :] for start in starts], axis=0)
            query = pieces[source * seq_size + k][c * SPAN : (c + 1) * SPAN, taken]
            grad = pieces[source * seq_size + k][tokens + c * SPAN : tokens + (c + 1) * SPAN, taken]
            reads.append((read[:, :HEAD_SIZE], read[:, HEAD_SIZE:]))
            queries.append(query)
            grad_rows.append(grad)
            scores.append(lax.dot_general(query, reads[-1][0], NT, preferred_element_type=jnp.float32))
            d_probs.append(lax.dot_general(grad, reads[-1][1], NT, preferred_element_type=jnp.float32))
        probs_low, d_scores = [], []
        for score, d_prob in zip(scores, d_probs):
            expos = jnp.exp(score * scale)
            probs = expos / jnp.sum(expos, axis=-1, keepdims=True)
            delta = jnp.sum(probs * d_prob, axis=-1, keepdims=True)
            probs_low.append(probs.astype(jnp.bfloat16))
            d_scores.append((probs * (d_prob - delta) * scale).astype(jnp.bfloat16))
        for n, (k, c, starts) in enumerate(spots):
            keys, values = reads[n]
            span = slice(c * SPAN, (c + 1) * SPAN)
            item_of(outs, k)[0, span, columns] = jnp.dot(
                probs_low[n], values, preferred_element_type=jnp.float32
            ).astype(jnp.bfloat16)
            item_of(outs, k)[1, span, columns] = jnp.dot(
                d_scores[n], keys, preferred_element_type=jnp.float32
            ).astype(jnp.bfloat16)
            d_keys = lax.dot_general(d_scores[n], queries[n], TN, preferred_element_type=jnp.float32)
            d_values = lax.dot_general(probs_low[n], grad_rows[n], TN, preferred_element_type=jnp.float32)
            both = jnp.concatenate([d_keys, d_values], axis=1)
            for r, start in enumerate(starts):
                d_kv[pl.ds(start, NLEN), wide] += both[r * NLEN : (r + 1) * NLEN]
    half = rows // 2
    for part in range(2):
        place = slice(part * half, (part + 1) * half)
        term = lax.dot_general(
            d_kv[place, :].astype(jnp.bfloat16), pair[...], NT, preferred_element_type=jnp.float32
        )
        if has_prior:
            term = term + prior[place, :].astype(jnp.float32)
        if last:
            grads[part][...] = term.astype(grads[part].dtype)
        else:
            grads[0][place, :] = term.astype(grads[0].dtype)


def attention(meta, stored, weights, takes, spans, prior, last):
    seq_size = len(stored)
    sources = []
    for source, _ in takes:
        if not any(source is known for known in sources):
            sources.append(source)
    takes = [([source is known for known in sources].index(True), at) for source, at in takes]
    pieces = [piece for source in sources for piece in source]
    block, width = stored[0].shape
    rows = seq_size * block
    count = len(weights) // 2
    prior = [] if prior is None else [prior]
    vmem = pl.BlockSpec(memory_space=pltpu.VMEM)
    operands = [*stored, *weights, *pieces, *prior]
    out_shape = bundles(seq_size, (2, spans * SPAN, count * HEAD_SIZE), jnp.bfloat16)
    levels = len(out_shape)
    if last:
        out_shape.append(jax.ShapeDtypeStruct((rows // 2, width), jnp.float32))
        out_shape.append(jax.ShapeDtypeStruct((rows // 2, width), jnp.bfloat16))
    else:
        out_shape.append(jax.ShapeDtypeStruct((rows, width), jnp.bfloat16))
    outs = pl.pallas_call(
        functools.partial(attention_body, seq_size, spans, takes, len(prior), last),
        out_shape=out_shape,
        in_specs=[pl.BlockSpec(memory_space=pltpu.SMEM)] + [vmem] * len(operands),
        out_specs=[vmem] * len(out_shape),
        scratch_shapes=[
            pltpu.VMEM((rows, width), jnp.bfloat16),
            pltpu.VMEM((width, 2 * count * HEAD_SIZE), jnp.bfloat16),
            pltpu.VMEM((rows, 2 * HEAD_SIZE), jnp.bfloat16),
            pltpu.VMEM((rows, 2 * count * HEAD_SIZE), jnp.float32),
        ],
        compiler_params=pltpu.CompilerParams(vmem_limit_bytes=vmem_bytes(rows)),
        cost_estimate=pl.CostEstimate(
            flops=count * 32 * rows * width * HEAD_SIZE, bytes_accessed=4 * rows * width, transcendentals=0
        ),
        name="attention",
    )(meta, *operands)
    return outs[:levels], outs[levels:]


def unpack_body(seq_size, groups, meta, *refs):
    count = len(groups) * seq_size
    attended, grad_queries = refs[count:]
    own, first = meta[0], meta[1]
    for g, heads in enumerate(groups):
        for k in range(seq_size):
            for i, r in enumerate(heads):
                column = pl.multiple_of(((first ^ r) * seq_size + (own ^ k)) * HEAD_SIZE, HEAD_SIZE)
                place = slice(i * HEAD_SIZE, (i + 1) * HEAD_SIZE)
                attended[0, :, pl.ds(column, HEAD_SIZE)] = refs[g * seq_size + k][0, :, place]
                grad_queries[0, :, pl.ds(column, HEAD_SIZE)] = refs[g * seq_size + k][1, :, place]


def unpack(meta, parts, groups, seq_size):
    tokens = parts[0].shape[1]
    shape = jax.ShapeDtypeStruct((1, tokens, HEADS * HEAD_SIZE), jnp.bfloat16)
    vmem = pl.BlockSpec(memory_space=pltpu.VMEM)
    return pl.pallas_call(
        functools.partial(unpack_body, seq_size, groups),
        out_shape=[shape, shape],
        in_specs=[pl.BlockSpec(memory_space=pltpu.SMEM)] + [vmem] * len(parts),
        out_specs=[vmem, vmem],
        compiler_params=pltpu.CompilerParams(vmem_limit_bytes=vmem_bytes(0)),
        name="unpack",
    )(meta, *parts)


def weight_slice(kv_weight, column):
    return lax.dynamic_slice_in_dim(kv_weight, column, HEAD_SIZE, axis=1)


def whole_weights(kv_weight, own, seq_size):
    whole = lax.all_gather(kv_weight, "dp", axis=1, tiled=True)
    pairs = []
    for r in range(HEADS // seq_size):
        column = (r * seq_size + own) * HEAD_SIZE
        pairs.append((weight_slice(whole, column), weight_slice(whole, column + HEADS * HEAD_SIZE)))
    return pairs


def tie(*values):
    return lax.optimization_barrier(values)


def per_device(dp_size, seq_size, queries, grad_out, encoded, kv_weight, neighbour_ids, slot_map):
    own = lax.axis_index("seq")
    place = lax.axis_index("dp")
    bits = seq_size.bit_length() - 1
    per_owner = encoded.shape[1]
    spans = neighbour_ids.shape[1]
    tokens = queries.shape[1]
    width = encoded.shape[3]
    pool_size = slot_map.shape[1]
    assert pool_size <= 256 and 1 << bits == seq_size
    split = dp_size == 8 and 2 * HEADS == dp_size * seq_size
    send = functools.partial(xor_send, axis="seq", size=seq_size)
    move = functools.partial(xor_send, axis="dp", size=dp_size)

    if split:
        first = place % (HEADS // seq_size)
        keys_first = (place < dp_size // 2).astype(jnp.int32)
        groups = [(0,), (1, 2), (3,)]
        packed = [(0, 1), (2, 3)]
    else:
        first, keys_first = place * 0, place * 0 + 1
        groups = packed = [tuple(range(HEADS // seq_size))]

    matches = neighbour_ids[0][:, :, None] == jnp.arange(pool_size, dtype=jnp.int32)[None, None, :]
    positions = jnp.sum(jnp.where(matches, slot_map[0][None, None, :], 0), axis=2).reshape(-1)
    head_meta = jnp.stack([own, first, keys_first, place])
    pieces = pack(jnp.concatenate([head_meta, positions]), queries, grad_out, packed, seq_size)
    early = exchange(pieces[0], seq_size)
    stored = [encoded[0].reshape(per_owner * NLEN, width)]
    for level in range(bits - 1, -1, -1):
        stored = stored + [send(rows, bit=1 << level) for rows in stored]
    positions = jnp.concatenate(
        [positions]
        + [piece[2 * tokens, : spans * READS].astype(jnp.int32) for piece in early[1:]]
    )
    relative = bit_reverse((positions // per_owner) ^ own, bits) * per_owner + positions % per_owner
    meta = jnp.concatenate([head_meta, relative])

    if split:
        mine = weight_slice(kv_weight, own * HEAD_SIZE)
        far, near, side = move(mine, bit=4), move(mine, bit=2), move(mine, bit=1)
        far, near, side, meta, early, stored, late = tie(far, near, side, meta, early, stored, pieces[1])
        near_far, side_far = move(far, bit=2), move(far, bit=1)
        late = exchange(late, seq_size)
        outs, (grads,) = attention(meta, stored, [mine, far], [(early, 0)], spans, None, False)
        parts = exchange(outs, seq_size)
        near_far, side_far, side, grads = tie(near_far, side_far, side, grads)
        side_near, side_near_far = move(side, bit=2), move(near_far, bit=1)
        late, parts, grads = tie(late, parts, grads)
        outs, (grads,) = attention(
            meta, stored, [side, side_far, near, near_far], [(early, 1), (late, 0)], spans, grads, False
        )
        parts = parts + exchange(outs, seq_size)
        outs, grads = attention(
            meta, stored, [side_near, side_near_far], [(late, 1)], spans, grads, True
        )
        parts = parts + exchange(outs, seq_size)
    else:
        weights = [block for pair in whole_weights(kv_weight, own, seq_size) for block in pair]
        takes = [(early, i) for i in range(HEADS // seq_size)]
        outs, grads = attention(meta, stored, weights, takes, spans, None, True)
        parts = exchange(outs, seq_size)
    total, leaving = grads
    for level in range(bits):
        total = total + send(leaving, bit=1 << level).astype(jnp.float32)
        half = total.shape[0] // 2
        if level < bits - 1:
            total, leaving = total[:half], total[half:].astype(jnp.bfloat16)
    attended, grad_queries = unpack(head_meta, parts, groups, seq_size)
    return attended, grad_queries, total.reshape(1, per_owner, NLEN, width)


def solution(mesh):
    in_specs = (
        P("dp", "seq", None),
        P("dp", "seq", None),
        P("dp", "seq", None, None),
        P(None, "dp"),
        P("dp", "seq", None),
        P("dp", None),
    )
    out_specs = (P("dp", "seq", None), P("dp", "seq", None), P("dp", "seq", None, None))
    return jax.shard_map(
        functools.partial(per_device, mesh.shape["dp"], mesh.shape["seq"]),
        mesh=mesh,
        in_specs=in_specs,
        out_specs=out_specs,
        check_vma=False,
    )
```

```python
import functools

import jax
import jax.numpy as jnp
from jax import lax
from jax.experimental import pallas as pl
from jax.experimental.pallas import tpu as pltpu
from jax.sharding import PartitionSpec as P

HEAD_SIZE = 128
HEADS = 16
SPAN = 64
NLEN = 64
READS = 2

NT = (((1,), (1,)), ((), ()))
TN = (((0,), (0,)), ((), ()))
EXTRA = 16
SMALL_BYTES = 4 << 20


def vmem_bytes(rows):
    return (3 << 20) + rows * (13 << 10)


def xor_send(value, axis, size, bit):
    return lax.ppermute(value, axis, [(i, i ^ bit) for i in range(size)])


def bit_reverse(index, bits):
    result = index * 0
    for i in range(bits):
        result = result + (((index >> i) & 1) << (bits - 1 - i))
    return result


def bundles(seq_size, item, dtype):
    sizes = [1] + [1 << b for b in range(seq_size.bit_length() - 1)]
    return [jax.ShapeDtypeStruct((size, *item), dtype) for size in sizes]


def item_of(refs, k):
    return refs[k.bit_length()].at[k - ((1 << k.bit_length()) >> 1)]


def cross(arrays, seq_size, top):
    return [*arrays[:top], xor_send(arrays[top], "seq", seq_size, 1 << (top - 1)), *arrays[top + 1 :]]


def forward(arrays, seq_size):
    top = len(arrays) - 1
    waiting = {b: [(0, array)] for b, array in enumerate(arrays[1:])}
    found = {0: (arrays[0], 0)}
    for b in reversed(range(top)):
        for origin, array in waiting[b]:
            arrived = array if b == top - 1 else xor_send(array, "seq", seq_size, 1 << b)
            origin = origin | (1 << b)
            found[origin] = (arrived, 0)
            for c in range(b):
                waiting[c].append((origin, arrived[1 << c : 2 << c]))
    return [found[j] for j in range(seq_size)]


def exchange(arrays, seq_size):
    return forward(cross(arrays, seq_size, len(arrays) - 1), seq_size)


def operands_of(items):
    arrays = []
    places = []
    for array, index in items:
        at = [array is known for known in arrays]
        if True not in at:
            at.append(True)
            arrays.append(array)
        places.append((at.index(True), index))
    return arrays, places


def pack_body(seq_size, groups, meta, ids, slots, queries, grad_out, *refs):
    held, sems = refs[-2], refs[-1]
    refs = refs[:-2]
    own, first = meta[0], meta[1]
    tokens = queries.shape[1]
    half = tokens // 2
    copies = []
    for part in range(2):
        for which, source in enumerate((queries, grad_out)):
            rows = pl.ds(part * half, half)
            copy = pltpu.make_async_copy(
                source.at[0, rows], held.at[which, rows], sems.at[2 * part + which]
            )
            copy.start()
            copies.append(copy)
    each = len(refs) // len(groups)
    spans = ids.shape[1]
    lanes = lax.broadcasted_iota(jnp.int32, (EXTRA, refs[0].shape[2]), 1)
    positions = jnp.zeros(lanes.shape, jnp.int32)
    for i in range(spans * READS):
        positions = jnp.where(lanes == i, slots[0, ids[0, i // READS, i % READS]], positions)
    positions = positions.astype(jnp.float32).astype(jnp.bfloat16)
    for k in range(seq_size):
        item_of(refs[:each], k)[2 * tokens :, :] = positions
    for part in range(2):
        for which in range(2):
            copies[2 * part + which].wait()
        rows = slice(part * half, (part + 1) * half)
        for g, heads in enumerate(groups):
            arrays = refs[g * each : (g + 1) * each]
            for k in range(seq_size):
                piece = item_of(arrays, k)
                for i, r in enumerate(heads):
                    column = pl.multiple_of(((first ^ r) * seq_size + (own ^ k)) * HEAD_SIZE, HEAD_SIZE)
                    place = slice(i * HEAD_SIZE, (i + 1) * HEAD_SIZE)
                    for which in range(2):
                        target = slice(which * tokens + rows.start, which * tokens + rows.stop)
                        piece[target, place] = held[which, rows, pl.ds(column, HEAD_SIZE)]


def pack(meta, neighbour_ids, slot_map, queries, grad_out, groups, seq_size):
    tokens, columns = queries.shape[1:]
    smem = pl.BlockSpec(memory_space=pltpu.SMEM)
    hbm = pl.BlockSpec(memory_space=pltpu.HBM)
    out_shape = []
    for g, heads in enumerate(groups):
        rows = 2 * tokens + (EXTRA if g == 0 else 0)
        out_shape += bundles(seq_size, (rows, len(heads) * HEAD_SIZE), jnp.bfloat16)
    outs = pl.pallas_call(
        functools.partial(pack_body, seq_size, groups),
        out_shape=out_shape,
        in_specs=[smem] * 3 + [hbm] * 2,
        out_specs=[pl.BlockSpec(memory_space=pltpu.VMEM)] * len(out_shape),
        scratch_shapes=[
            pltpu.VMEM((2, tokens, columns), jnp.bfloat16),
            pltpu.SemaphoreType.DMA((4,)),
        ],
        compiler_params=pltpu.CompilerParams(vmem_limit_bytes=SMALL_BYTES),
        cost_estimate=pl.CostEstimate(flops=0, bytes_accessed=0, transcendentals=0),
        name="pack",
    )(meta, neighbour_ids, slot_map, queries, grad_out)
    each = len(outs) // len(groups)
    return [outs[g * each : (g + 1) * each] for g in range(len(groups))]


def relative_positions(pieces, own, per_owner, tokens):
    bits = len(pieces).bit_length() - 1
    shift = per_owner.bit_length() - 1
    rows = [piece[2 * tokens : 2 * tokens + 8, :HEAD_SIZE] for piece in pieces]
    out = []
    for row in rows:
        position = row.astype(jnp.float32).astype(jnp.int32)
        owner = bit_reverse((position >> shift) ^ own, bits)
        out.append((owner << shift) + (position & (per_owner - 1)))
    return out


def attention_body(seq_size, spans, takes, places, arrays, per_owner, finds, has_prior, last, *refs):
    count = len(takes)
    meta, refs = refs[0], refs[1:]
    table, refs = (None, refs) if finds else (refs[0], refs[1:])
    stored, refs = refs[:seq_size], refs[seq_size:]
    weights, refs = refs[: 2 * count], refs[2 * count :]
    pieces, refs = refs[:arrays], refs[arrays:]
    pieces = [pieces[at].at[index] for at, index in places]
    prior, refs = (refs[0], refs[1:]) if has_prior else (None, refs)
    levels = seq_size.bit_length()
    outs, refs = refs[:levels], refs[levels:]
    grads, refs = (refs[:2], refs[2:]) if last else (refs[:1], refs[1:])
    if finds:
        found, refs = refs[0], refs[1:]
    enc, pair, kv, d_kv = refs[:4]
    block = stored[0].shape[0]
    rows = enc.shape[0]
    tokens = spans * SPAN
    scale = HEAD_SIZE ** (-0.5)
    keys_first = meta[2] == 1
    for i in range(seq_size):
        enc[i * block : (i + 1) * block] = stored[i][...]
    if finds:
        for k, rows_of in enumerate(relative_positions(pieces[:seq_size], meta[0], per_owner, tokens)):
            found[8 * k : 8 * k + 8, :] = rows_of
        table, sem = refs[4:]
        copy = pltpu.make_async_copy(found, table, sem)
        copy.start()
        copy.wait()
    spots = []
    for k in range(seq_size):
        for c in range(spans):
            starts = [table[8 * k, c * READS + r] * NLEN for r in range(READS)]
            spots.append((k, c, [pl.multiple_of(start, NLEN) for start in starts]))
    for i in range(count):
        first, second = weights[2 * i][...], weights[2 * i + 1][...]
        wide = slice(2 * i * HEAD_SIZE, 2 * (i + 1) * HEAD_SIZE)
        pair[:, 2 * i * HEAD_SIZE : (2 * i + 1) * HEAD_SIZE] = jnp.where(keys_first, first, second)
        pair[:, (2 * i + 1) * HEAD_SIZE : (2 * i + 2) * HEAD_SIZE] = jnp.where(keys_first, second, first)
        kv[...] = jnp.dot(enc[...], pair[:, wide], preferred_element_type=jnp.float32).astype(jnp.bfloat16)
        d_kv[:, wide] = jnp.zeros((rows, 2 * HEAD_SIZE), jnp.float32)
        columns = slice(i * HEAD_SIZE, (i + 1) * HEAD_SIZE)
        source, at = takes[i]
        taken = slice(at * HEAD_SIZE, (at + 1) * HEAD_SIZE)
        reads, queries, grad_rows, scores, d_probs = [], [], [], [], []
        for k, c, starts in spots:
            read = jnp.concatenate([kv[pl.ds(start, NLEN), :] for start in starts], axis=0)
            query = pieces[source * seq_size + k][c * SPAN : (c + 1) * SPAN, taken]
            grad = pieces[source * seq_size + k][tokens + c * SPAN : tokens + (c + 1) * SPAN, taken]
            reads.append((read[:, :HEAD_SIZE], read[:, HEAD_SIZE:]))
            queries.append(query)
            grad_rows.append(grad)
            scores.append(lax.dot_general(query, reads[-1][0], NT, preferred_element_type=jnp.float32))
            d_probs.append(lax.dot_general(grad, reads[-1][1], NT, preferred_element_type=jnp.float32))
        probs_low, d_scores = [], []
        for score, d_prob in zip(scores, d_probs):
            expos = jnp.exp(score * scale)
            probs = expos / jnp.sum(expos, axis=-1, keepdims=True)
            delta = jnp.sum(probs * d_prob, axis=-1, keepdims=True)
            probs_low.append(probs.astype(jnp.bfloat16))
            d_scores.append((probs * (d_prob - delta) * scale).astype(jnp.bfloat16))
        for n, (k, c, starts) in enumerate(spots):
            keys, values = reads[n]
            span = slice(c * SPAN, (c + 1) * SPAN)
            item_of(outs, k)[0, span, columns] = jnp.dot(
                probs_low[n], values, preferred_element_type=jnp.float32
            ).astype(jnp.bfloat16)
            item_of(outs, k)[1, span, columns] = jnp.dot(
                d_scores[n], keys, preferred_element_type=jnp.float32
            ).astype(jnp.bfloat16)
            d_keys = lax.dot_general(d_scores[n], queries[n], TN, preferred_element_type=jnp.float32)
            d_values = lax.dot_general(probs_low[n], grad_rows[n], TN, preferred_element_type=jnp.float32)
            both = jnp.concatenate([d_keys, d_values], axis=1)
            for r, start in enumerate(starts):
                d_kv[pl.ds(start, NLEN), wide] += both[r * NLEN : (r + 1) * NLEN]
    half = rows // 2
    for part in range(2):
        place = slice(part * half, (part + 1) * half)
        term = lax.dot_general(
            d_kv[place, :].astype(jnp.bfloat16), pair[...], NT, preferred_element_type=jnp.float32
        )
        if has_prior:
            term = term + prior[place, :].astype(jnp.float32)
        if last:
            grads[part][...] = term.astype(grads[part].dtype)
        else:
            grads[0][place, :] = term.astype(grads[0].dtype)


def attention(meta, table, stored, weights, takes, spans, per_owner, prior, last):
    seq_size = len(stored)
    sources = []
    for source, _ in takes:
        if not any(source is known for known in sources):
            sources.append(source)
    takes = [([source is known for known in sources].index(True), at) for source, at in takes]
    arrays, places = operands_of([item for source in sources for item in source])
    block, width = stored[0].shape
    rows = seq_size * block
    count = len(weights) // 2
    prior = [] if prior is None else [prior]
    vmem = pl.BlockSpec(memory_space=pltpu.VMEM)
    operands = [*stored, *weights, *arrays, *prior]
    finds = table is None
    scalars = [meta] if finds else [meta, table]
    table_shape = (8 * seq_size, HEAD_SIZE)
    out_shape = bundles(seq_size, (2, spans * SPAN, count * HEAD_SIZE), jnp.bfloat16)
    levels = len(out_shape)
    if last:
        out_shape.append(jax.ShapeDtypeStruct((rows // 2, width), jnp.float32))
        out_shape.append(jax.ShapeDtypeStruct((rows // 2, width), jnp.bfloat16))
    else:
        out_shape.append(jax.ShapeDtypeStruct((rows, width), jnp.bfloat16))
    grads = len(out_shape) - levels
    scratch = [
        pltpu.VMEM((rows, width), jnp.bfloat16),
        pltpu.VMEM((width, 2 * count * HEAD_SIZE), jnp.bfloat16),
        pltpu.VMEM((rows, 2 * HEAD_SIZE), jnp.bfloat16),
        pltpu.VMEM((rows, 2 * count * HEAD_SIZE), jnp.float32),
    ]
    if finds:
        out_shape.append(jax.ShapeDtypeStruct(table_shape, jnp.int32))
        scratch += [pltpu.SMEM(table_shape, jnp.int32), pltpu.SemaphoreType.DMA]
    outs = pl.pallas_call(
        functools.partial(
            attention_body, seq_size, spans, takes, places, len(arrays), per_owner, finds, len(prior), last
        ),
        out_shape=out_shape,
        in_specs=[pl.BlockSpec(memory_space=pltpu.SMEM)] * len(scalars) + [vmem] * len(operands),
        out_specs=[vmem] * len(out_shape),
        scratch_shapes=scratch,
        compiler_params=pltpu.CompilerParams(vmem_limit_bytes=vmem_bytes(rows)),
        cost_estimate=pl.CostEstimate(
            flops=0, bytes_accessed=0, transcendentals=0
        ),
        name="attention",
    )(*scalars, *operands)
    return outs[:levels], outs[levels : levels + grads], outs[-1] if finds else table


def unpack_body(seq_size, groups, places, meta, *refs):
    attended, grad_queries = refs[-2:]
    own, first = meta[0], meta[1]
    for g, heads in enumerate(groups):
        for k in range(seq_size):
            at, index = places[g * seq_size + k]
            for i, r in enumerate(heads):
                column = pl.multiple_of(((first ^ r) * seq_size + (own ^ k)) * HEAD_SIZE, HEAD_SIZE)
                place = slice(i * HEAD_SIZE, (i + 1) * HEAD_SIZE)
                attended[0, :, pl.ds(column, HEAD_SIZE)] = refs[at][index, 0, :, place]
                grad_queries[0, :, pl.ds(column, HEAD_SIZE)] = refs[at][index, 1, :, place]


def unpack(meta, items, groups, seq_size):
    arrays, places = operands_of(items)
    tokens = arrays[0].shape[2]
    shape = jax.ShapeDtypeStruct((1, tokens, HEADS * HEAD_SIZE), jnp.bfloat16)
    vmem = pl.BlockSpec(memory_space=pltpu.VMEM)
    return pl.pallas_call(
        functools.partial(unpack_body, seq_size, groups, places),
        out_shape=[shape, shape],
        in_specs=[pl.BlockSpec(memory_space=pltpu.SMEM)] + [vmem] * len(arrays),
        out_specs=[vmem, vmem],
        compiler_params=pltpu.CompilerParams(vmem_limit_bytes=SMALL_BYTES),
        cost_estimate=pl.CostEstimate(flops=0, bytes_accessed=0, transcendentals=0),
        name="unpack",
    )(meta, *arrays)


def weight_slice(kv_weight, column):
    return lax.dynamic_slice_in_dim(kv_weight, column, HEAD_SIZE, axis=1)


def whole_weights(kv_weight, own, seq_size):
    whole = lax.all_gather(kv_weight, "dp", axis=1, tiled=True)
    pairs = []
    for r in range(HEADS // seq_size):
        column = (r * seq_size + own) * HEAD_SIZE
        pairs.append((weight_slice(whole, column), weight_slice(whole, column + HEADS * HEAD_SIZE)))
    return pairs


def tie(*values):
    return lax.optimization_barrier(values)


def per_device(dp_size, seq_size, queries, grad_out, encoded, kv_weight, neighbour_ids, slot_map):
    own = lax.axis_index("seq")
    place = lax.axis_index("dp")
    bits = seq_size.bit_length() - 1
    per_owner = encoded.shape[1]
    spans = neighbour_ids.shape[1]
    tokens = queries.shape[1]
    width = encoded.shape[3]
    pool_size = slot_map.shape[1]
    assert pool_size <= 256 and 1 << bits == seq_size and per_owner & (per_owner - 1) == 0
    split = dp_size == 8 and 2 * HEADS == dp_size * seq_size
    send = functools.partial(xor_send, axis="seq", size=seq_size)
    move = functools.partial(xor_send, axis="dp", size=dp_size)

    if split:
        first = place % (HEADS // seq_size)
        keys_first = (place < dp_size // 2).astype(jnp.int32)
        groups = [(0,), (1, 2), (3,)]
        packed = [(0,), (1, 2, 3)]
    else:
        first, keys_first = place * 0, place * 0 + 1
        groups = packed = [tuple(range(HEADS // seq_size))]

    head_meta = jnp.stack([own, first, keys_first, place])
    pieces = pack(head_meta, neighbour_ids, slot_map, queries, grad_out, packed, seq_size)
    stored = [encoded[0].reshape(per_owner * NLEN, width)]
    if not split:
        for level in range(bits - 1, -1, -1):
            stored = stored + [send(rows, bit=1 << level) for rows in stored]
    if split:
        mine = weight_slice(kv_weight, own * HEAD_SIZE)
        stored = stored + [send(stored[0], bit=2)]
        stored = stored + [send(rows, bit=1) for rows in stored]
        early = cross(pieces[0], seq_size, bits)
        far, near, side, stored, early = tie(
            move(mine, bit=4), move(mine, bit=2), move(mine, bit=1), stored, early
        )
        near_far, side_far = move(far, bit=2), move(far, bit=1)
        early = forward(early, seq_size)
        late = cross(pieces[1], seq_size, bits)
        attend = functools.partial(attention, head_meta, spans=spans, per_owner=per_owner)
        outs, (grads,), table = attend(
            None, stored, [mine, far], [(early, 0)], prior=None, last=False
        )
        parts_a = cross(outs, seq_size, bits)
        near_far, side_far, side, near, late, grads = tie(near_far, side_far, side, near, late, grads)
        side_near_far, side_near = move(near_far, bit=1), move(side, bit=2)
        late = forward(late, seq_size)
        outs, (grads,), _ = attend(
            table, stored, [side, side_far, near, near_far], [(late, 0), (late, 1)], prior=grads, last=False
        )
        parts_b = cross(outs, seq_size, bits)
        grads, parts_a = tie(grads, parts_a)
        outs, grads, _ = attend(
            table, stored, [side_near, side_near_far], [(late, 2)], prior=grads, last=True
        )
        parts_b, parts_c = tie(parts_b, cross(outs, seq_size, bits))
        items = [item for parts in (parts_a, parts_b, parts_c) for item in forward(parts, seq_size)]
    else:
        weights = [block for pair in whole_weights(kv_weight, own, seq_size) for block in pair]
        early = exchange(pieces[0], seq_size)
        takes = [(early, i) for i in range(HEADS // seq_size)]
        outs, grads, _ = attention(head_meta, None, stored, weights, takes, spans, per_owner, None, True)
        items = exchange(outs, seq_size)
    total, leaving = grads
    for level in range(bits):
        total = total + send(leaving, bit=1 << level).astype(jnp.float32)
        half = total.shape[0] // 2
        if level < bits - 1:
            total, leaving = total[:half], total[half:].astype(jnp.bfloat16)
    attended, grad_queries = unpack(head_meta, items, groups, seq_size)
    return attended, grad_queries, total.reshape(1, per_owner, NLEN, width)


def solution(mesh):
    in_specs = (
        P("dp", "seq", None),
        P("dp", "seq", None),
        P("dp", "seq", None, None),
        P(None, "dp"),
        P("dp", "seq", None),
        P("dp", None),
    )
    out_specs = (P("dp", "seq", None), P("dp", "seq", None), P("dp", "seq", None, None))
    return jax.shard_map(
        functools.partial(per_device, mesh.shape["dp"], mesh.shape["seq"]),
        mesh=mesh,
        in_specs=in_specs,
        out_specs=out_specs,
        check_vma=False,
    )
```

```python
import functools

import jax
import jax.numpy as jnp
from jax import lax
from jax.experimental import pallas as pl
from jax.experimental.pallas import tpu as pltpu
from jax.sharding import PartitionSpec as P

HEAD_SIZE = 128
HEADS = 16
SPAN = 64
NLEN = 64
READS = 2

NT = (((1,), (1,)), ((), ()))
TN = (((0,), (0,)), ((), ()))
EXTRA = 16
SMALL_BYTES = 4 << 20


def vmem_bytes(rows):
    return (3 << 20) + rows * (13 << 10)


def xor_send(value, axis, size, bit):
    return lax.ppermute(value, axis, [(i, i ^ bit) for i in range(size)])


def bit_reverse(index, bits):
    result = index * 0
    for i in range(bits):
        result = result + (((index >> i) & 1) << (bits - 1 - i))
    return result


def bundles(seq_size, item, dtype):
    sizes = [1] + [1 << b for b in range(seq_size.bit_length() - 1)]
    return [jax.ShapeDtypeStruct((size, *item), dtype) for size in sizes]


def item_of(refs, k):
    return refs[k.bit_length()].at[k - ((1 << k.bit_length()) >> 1)]


def cross(arrays, seq_size, top):
    return [*arrays[:top], xor_send(arrays[top], "seq", seq_size, 1 << (top - 1)), *arrays[top + 1 :]]


def forward(arrays, seq_size):
    top = len(arrays) - 1
    waiting = {b: [(0, array)] for b, array in enumerate(arrays[1:])}
    found = {0: (arrays[0], 0)}
    for b in reversed(range(top)):
        for origin, array in waiting[b]:
            arrived = array if b == top - 1 else xor_send(array, "seq", seq_size, 1 << b)
            origin = origin | (1 << b)
            found[origin] = (arrived, 0)
            for c in range(b):
                waiting[c].append((origin, arrived[1 << c : 2 << c]))
    return [found[j] for j in range(seq_size)]


def exchange(arrays, seq_size):
    return forward(cross(arrays, seq_size, len(arrays) - 1), seq_size)


def operands_of(items):
    arrays = []
    places = []
    for array, index in items:
        at = [array is known for known in arrays]
        if True not in at:
            at.append(True)
            arrays.append(array)
        places.append((at.index(True), index))
    return arrays, places


def pack_body(seq_size, groups, meta, ids, slots, queries, grad_out, *refs):
    held, sems = refs[-2], refs[-1]
    refs = refs[:-2]
    own, first = meta[0], meta[1]
    tokens = queries.shape[1]
    half = tokens // 2
    copies = []
    for part in range(2):
        for which, source in enumerate((queries, grad_out)):
            rows = pl.ds(part * half, half)
            copy = pltpu.make_async_copy(
                source.at[0, rows], held.at[which, rows], sems.at[2 * part + which]
            )
            copy.start()
            copies.append(copy)
    each = len(refs) // len(groups)
    spans = ids.shape[1]
    lanes = lax.broadcasted_iota(jnp.int32, (EXTRA, refs[0].shape[2]), 1)
    positions = jnp.zeros(lanes.shape, jnp.int32)
    for i in range(spans * READS):
        positions = jnp.where(lanes == i, slots[0, ids[0, i // READS, i % READS]], positions)
    positions = positions.astype(jnp.float32).astype(jnp.bfloat16)
    for k in range(seq_size):
        item_of(refs[:each], k)[2 * tokens :, :] = positions
    for part in range(2):
        for which in range(2):
            copies[2 * part + which].wait()
        rows = slice(part * half, (part + 1) * half)
        for g, heads in enumerate(groups):
            arrays = refs[g * each : (g + 1) * each]
            for k in range(seq_size):
                piece = item_of(arrays, k)
                for i, r in enumerate(heads):
                    column = pl.multiple_of(((first ^ r) * seq_size + (own ^ k)) * HEAD_SIZE, HEAD_SIZE)
                    place = slice(i * HEAD_SIZE, (i + 1) * HEAD_SIZE)
                    for which in range(2):
                        target = slice(which * tokens + rows.start, which * tokens + rows.stop)
                        piece[target, place] = held[which, rows, pl.ds(column, HEAD_SIZE)]


def pack(meta, neighbour_ids, slot_map, queries, grad_out, groups, seq_size):
    tokens, columns = queries.shape[1:]
    smem = pl.BlockSpec(memory_space=pltpu.SMEM)
    hbm = pl.BlockSpec(memory_space=pltpu.HBM)
    out_shape = []
    for g, heads in enumerate(groups):
        rows = 2 * tokens + (EXTRA if g == 0 else 0)
        out_shape += bundles(seq_size, (rows, len(heads) * HEAD_SIZE), jnp.bfloat16)
    outs = pl.pallas_call(
        functools.partial(pack_body, seq_size, groups),
        out_shape=out_shape,
        in_specs=[smem] * 3 + [hbm] * 2,
        out_specs=[pl.BlockSpec(memory_space=pltpu.VMEM)] * len(out_shape),
        scratch_shapes=[
            pltpu.VMEM((2, tokens, columns), jnp.bfloat16),
            pltpu.SemaphoreType.DMA((4,)),
        ],
        compiler_params=pltpu.CompilerParams(vmem_limit_bytes=SMALL_BYTES),
        cost_estimate=pl.CostEstimate(flops=0, bytes_accessed=0, transcendentals=0),
        name="pack",
    )(meta, neighbour_ids, slot_map, queries, grad_out)
    each = len(outs) // len(groups)
    return [outs[g * each : (g + 1) * each] for g in range(len(groups))]


def relative_positions(pieces, own, per_owner, tokens):
    bits = len(pieces).bit_length() - 1
    shift = per_owner.bit_length() - 1
    rows = [piece[2 * tokens : 2 * tokens + 8, :HEAD_SIZE] for piece in pieces]
    out = []
    for row in rows:
        position = row.astype(jnp.float32).astype(jnp.int32)
        owner = bit_reverse((position >> shift) ^ own, bits)
        out.append((owner << shift) + (position & (per_owner - 1)))
    return out


def attention_body(seq_size, spans, takes, places, arrays, per_owner, finds, has_prior, last, *refs):
    count = len(takes)
    meta, refs = refs[0], refs[1:]
    table, refs = (None, refs) if finds else (refs[0], refs[1:])
    stored, refs = refs[:seq_size], refs[seq_size:]
    weights, refs = refs[: 2 * count], refs[2 * count :]
    pieces, refs = refs[:arrays], refs[arrays:]
    pieces = [pieces[at].at[index] for at, index in places]
    prior, refs = (refs[0], refs[1:]) if has_prior else (None, refs)
    levels = seq_size.bit_length()
    outs, refs = refs[:levels], refs[levels:]
    grads, refs = (refs[:2], refs[2:]) if last else (refs[:1], refs[1:])
    if finds:
        found, refs = refs[0], refs[1:]
    enc, pair, kv, d_kv = refs[:4]
    block = stored[0].shape[0]
    rows = enc.shape[0]
    tokens = spans * SPAN
    scale = HEAD_SIZE ** (-0.5)
    keys_first = meta[2] == 1
    for i in range(seq_size):
        enc[i * block : (i + 1) * block] = stored[i][...]
    if finds:
        for k, rows_of in enumerate(relative_positions(pieces[:seq_size], meta[0], per_owner, tokens)):
            found[8 * k : 8 * k + 8, :] = rows_of
        table, sem = refs[4:]
        copy = pltpu.make_async_copy(found, table, sem)
        copy.start()
        copy.wait()
    spots = []
    for k in range(seq_size):
        for c in range(spans):
            starts = [table[8 * k, c * READS + r] * NLEN for r in range(READS)]
            spots.append((k, c, [pl.multiple_of(start, NLEN) for start in starts]))
    for i in range(count):
        first, second = weights[2 * i][...], weights[2 * i + 1][...]
        wide = slice(2 * i * HEAD_SIZE, 2 * (i + 1) * HEAD_SIZE)
        pair[:, 2 * i * HEAD_SIZE : (2 * i + 1) * HEAD_SIZE] = jnp.where(keys_first, first, second)
        pair[:, (2 * i + 1) * HEAD_SIZE : (2 * i + 2) * HEAD_SIZE] = jnp.where(keys_first, second, first)
        kv[...] = jnp.dot(enc[...], pair[:, wide], preferred_element_type=jnp.float32).astype(jnp.bfloat16)
        d_kv[:, wide] = jnp.zeros((rows, 2 * HEAD_SIZE), jnp.float32)
        columns = slice(i * HEAD_SIZE, (i + 1) * HEAD_SIZE)
        source, at = takes[i]
        taken = slice(at * HEAD_SIZE, (at + 1) * HEAD_SIZE)
        reads, queries, grad_rows, scores, d_probs = [], [], [], [], []
        for k, c, starts in spots:
            read = jnp.concatenate([kv[pl.ds(start, NLEN), :] for start in starts], axis=0)
            query = pieces[source * seq_size + k][c * SPAN : (c + 1) * SPAN, taken]
            grad = pieces[source * seq_size + k][tokens + c * SPAN : tokens + (c + 1) * SPAN, taken]
            reads.append((read[:, :HEAD_SIZE], read[:, HEAD_SIZE:]))
            queries.append(query)
            grad_rows.append(grad)
            scores.append(lax.dot_general(query, reads[-1][0], NT, preferred_element_type=jnp.float32))
            d_probs.append(lax.dot_general(grad, reads[-1][1], NT, preferred_element_type=jnp.float32))
        probs_low, d_scores = [], []
        for score, d_prob in zip(scores, d_probs):
            expos = jnp.exp(score * scale)
            probs = expos / jnp.sum(expos, axis=-1, keepdims=True)
            delta = jnp.sum(probs * d_prob, axis=-1, keepdims=True)
            probs_low.append(probs.astype(jnp.bfloat16))
            d_scores.append((probs * (d_prob - delta) * scale).astype(jnp.bfloat16))
        for n, (k, c, starts) in enumerate(spots):
            keys, values = reads[n]
            span = slice(c * SPAN, (c + 1) * SPAN)
            item_of(outs, k)[0, span, columns] = jnp.dot(
                probs_low[n], values, preferred_element_type=jnp.float32
            ).astype(jnp.bfloat16)
            item_of(outs, k)[1, span, columns] = jnp.dot(
                d_scores[n], keys, preferred_element_type=jnp.float32
            ).astype(jnp.bfloat16)
            d_keys = lax.dot_general(d_scores[n], queries[n], TN, preferred_element_type=jnp.float32)
            d_values = lax.dot_general(probs_low[n], grad_rows[n], TN, preferred_element_type=jnp.float32)
            both = jnp.concatenate([d_keys, d_values], axis=1)
            for r, start in enumerate(starts):
                d_kv[pl.ds(start, NLEN), wide] += both[r * NLEN : (r + 1) * NLEN]
    half = rows // 2
    for part in range(2):
        place = slice(part * half, (part + 1) * half)
        term = lax.dot_general(
            d_kv[place, :].astype(jnp.bfloat16), pair[...], NT, preferred_element_type=jnp.float32
        )
        if has_prior:
            term = term + prior[place, :].astype(jnp.float32)
        if last:
            grads[part][...] = term.astype(grads[part].dtype)
        else:
            grads[0][place, :] = term.astype(grads[0].dtype)


def attention(meta, table, stored, weights, takes, spans, per_owner, prior, last):
    seq_size = len(stored)
    sources = []
    for source, _ in takes:
        if not any(source is known for known in sources):
            sources.append(source)
    takes = [([source is known for known in sources].index(True), at) for source, at in takes]
    arrays, places = operands_of([item for source in sources for item in source])
    block, width = stored[0].shape
    rows = seq_size * block
    count = len(weights) // 2
    prior = [] if prior is None else [prior]
    vmem = pl.BlockSpec(memory_space=pltpu.VMEM)
    operands = [*stored, *weights, *arrays, *prior]
    finds = table is None
    scalars = [meta] if finds else [meta, table]
    table_shape = (8 * seq_size, HEAD_SIZE)
    out_shape = bundles(seq_size, (2, spans * SPAN, count * HEAD_SIZE), jnp.bfloat16)
    levels = len(out_shape)
    if last:
        out_shape.append(jax.ShapeDtypeStruct((rows // 2, width), jnp.float32))
        out_shape.append(jax.ShapeDtypeStruct((rows // 2, width), jnp.bfloat16))
    else:
        out_shape.append(jax.ShapeDtypeStruct((rows, width), jnp.bfloat16))
    grads = len(out_shape) - levels
    scratch = [
        pltpu.VMEM((rows, width), jnp.bfloat16),
        pltpu.VMEM((width, 2 * count * HEAD_SIZE), jnp.bfloat16),
        pltpu.VMEM((rows, 2 * HEAD_SIZE), jnp.bfloat16),
        pltpu.VMEM((rows, 2 * count * HEAD_SIZE), jnp.float32),
    ]
    if finds:
        out_shape.append(jax.ShapeDtypeStruct(table_shape, jnp.int32))
        scratch += [pltpu.SMEM(table_shape, jnp.int32), pltpu.SemaphoreType.DMA]
    outs = pl.pallas_call(
        functools.partial(
            attention_body, seq_size, spans, takes, places, len(arrays), per_owner, finds, len(prior), last
        ),
        out_shape=out_shape,
        in_specs=[pl.BlockSpec(memory_space=pltpu.SMEM)] * len(scalars) + [vmem] * len(operands),
        out_specs=[vmem] * len(out_shape),
        scratch_shapes=scratch,
        compiler_params=pltpu.CompilerParams(vmem_limit_bytes=vmem_bytes(rows)),
        cost_estimate=pl.CostEstimate(
            flops=int(2.4e9) if last and len(prior) else 0, bytes_accessed=0, transcendentals=0
        ),
        name="attention",
    )(*scalars, *operands)
    return outs[:levels], outs[levels : levels + grads], outs[-1] if finds else table


def unpack_body(seq_size, groups, places, meta, *refs):
    attended, grad_queries = refs[-2:]
    own, first = meta[0], meta[1]
    for g, heads in enumerate(groups):
        for k in range(seq_size):
            at, index = places[g * seq_size + k]
            for i, r in enumerate(heads):
                column = pl.multiple_of(((first ^ r) * seq_size + (own ^ k)) * HEAD_SIZE, HEAD_SIZE)
                place = slice(i * HEAD_SIZE, (i + 1) * HEAD_SIZE)
                attended[0, :, pl.ds(column, HEAD_SIZE)] = refs[at][index, 0, :, place]
                grad_queries[0, :, pl.ds(column, HEAD_SIZE)] = refs[at][index, 1, :, place]


def unpack(meta, items, groups, seq_size):
    arrays, places = operands_of(items)
    tokens = arrays[0].shape[2]
    shape = jax.ShapeDtypeStruct((1, tokens, HEADS * HEAD_SIZE), jnp.bfloat16)
    vmem = pl.BlockSpec(memory_space=pltpu.VMEM)
    return pl.pallas_call(
        functools.partial(unpack_body, seq_size, groups, places),
        out_shape=[shape, shape],
        in_specs=[pl.BlockSpec(memory_space=pltpu.SMEM)] + [vmem] * len(arrays),
        out_specs=[vmem, vmem],
        compiler_params=pltpu.CompilerParams(vmem_limit_bytes=SMALL_BYTES),
        cost_estimate=pl.CostEstimate(flops=0, bytes_accessed=0, transcendentals=0),
        name="unpack",
    )(meta, *arrays)


def weight_slice(kv_weight, column):
    return lax.dynamic_slice_in_dim(kv_weight, column, HEAD_SIZE, axis=1)


def whole_weights(kv_weight, own, seq_size):
    whole = lax.all_gather(kv_weight, "dp", axis=1, tiled=True)
    pairs = []
    for r in range(HEADS // seq_size):
        column = (r * seq_size + own) * HEAD_SIZE
        pairs.append((weight_slice(whole, column), weight_slice(whole, column + HEADS * HEAD_SIZE)))
    return pairs


def tie(*values):
    return lax.optimization_barrier(values)


def fold(total, arrived):
    total = total + arrived.astype(jnp.float32)
    half = total.shape[0] // 2
    return total[:half], total[half:].astype(jnp.bfloat16)


def tie_items(value, items):
    tied = lax.optimization_barrier((value, [array for array, _ in items]))
    return tied[0], [(array, index) for array, (_, index) in zip(tied[1], items)]


def per_device(dp_size, seq_size, queries, grad_out, encoded, kv_weight, neighbour_ids, slot_map):
    own = lax.axis_index("seq")
    place = lax.axis_index("dp")
    bits = seq_size.bit_length() - 1
    per_owner = encoded.shape[1]
    spans = neighbour_ids.shape[1]
    tokens = queries.shape[1]
    width = encoded.shape[3]
    pool_size = slot_map.shape[1]
    assert pool_size <= 256 and 1 << bits == seq_size and per_owner & (per_owner - 1) == 0
    split = dp_size == 8 and 2 * HEADS == dp_size * seq_size
    send = functools.partial(xor_send, axis="seq", size=seq_size)
    move = functools.partial(xor_send, axis="dp", size=dp_size)

    if split:
        first = place % (HEADS // seq_size)
        keys_first = (place < dp_size // 2).astype(jnp.int32)
        groups = [(0,), (1, 2), (3,)]
        packed = [(0,), (1, 2, 3)]
    else:
        first, keys_first = place * 0, place * 0 + 1
        groups = packed = [tuple(range(HEADS // seq_size))]

    head_meta = jnp.stack([own, first, keys_first, place])
    pieces = pack(head_meta, neighbour_ids, slot_map, queries, grad_out, packed, seq_size)
    stored = [encoded[0].reshape(per_owner * NLEN, width)]
    if not split:
        for level in range(bits - 1, -1, -1):
            stored = stored + [send(rows, bit=1 << level) for rows in stored]
    if split:
        mine = weight_slice(kv_weight, own * HEAD_SIZE)
        stored = stored + [send(stored[0], bit=2)]
        stored = stored + [send(rows, bit=1) for rows in stored]
        early = cross(pieces[0], seq_size, bits)
        far, near, side, late = tie(move(mine, bit=4), move(mine, bit=2), move(mine, bit=1), pieces[1])
        near_far = move(far, bit=2)
        side_far = move(far, bit=1)
        early = forward(early, seq_size)
        late = cross(late, seq_size, bits)
        attend = functools.partial(attention, head_meta, spans=spans, per_owner=per_owner)
        outs, (grads,), table = attend(
            None, stored, [mine, far], [(early, 0)], prior=None, last=False
        )
        near_far, outs = tie(near_far, outs)
        parts_a = cross(outs, seq_size, bits)
        near_far, side_far, side, near, late, grads = tie(near_far, side_far, side, near, late, grads)
        side_near_far, side_near = move(near_far, bit=1), move(side, bit=2)
        late = forward(late, seq_size)
        outs, (grads,), _ = attend(
            table, stored, [side, side_far, near, near_far], [(late, 0), (late, 1)], prior=grads, last=False
        )
        parts_b = cross(outs, seq_size, bits)
        grads, parts_a = tie(grads, parts_a)
        outs, grads, _ = attend(
            table, stored, [side_near, side_near_far], [(late, 2)], prior=grads, last=True
        )
        parts_c = cross(outs, seq_size, bits)
        grads, parts_b = tie(grads, parts_b)
        total, leaving = fold(grads[0], send(grads[1], bit=1))
        items = [item for parts in (parts_a, parts_b, parts_c) for item in forward(parts, seq_size)]
    else:
        weights = [block for pair in whole_weights(kv_weight, own, seq_size) for block in pair]
        early = exchange(pieces[0], seq_size)
        takes = [(early, i) for i in range(HEADS // seq_size)]
        outs, grads, _ = attention(head_meta, None, stored, weights, takes, spans, per_owner, None, True)
        items = exchange(outs, seq_size)
    if not split:
        total, leaving = grads
        for level in range(bits - 1):
            total, leaving = fold(total, send(leaving, bit=1 << level))
    total = total + send(leaving, bit=1 << (bits - 1)).astype(jnp.float32)
    attended, grad_queries = unpack(head_meta, items, groups, seq_size)
    return attended, grad_queries, total.reshape(1, per_owner, NLEN, width)


def solution(mesh):
    in_specs = (
        P("dp", "seq", None),
        P("dp", "seq", None),
        P("dp", "seq", None, None),
        P(None, "dp"),
        P("dp", "seq", None),
        P("dp", None),
    )
    out_specs = (P("dp", "seq", None), P("dp", "seq", None), P("dp", "seq", None, None))
    return jax.shard_map(
        functools.partial(per_device, mesh.shape["dp"], mesh.shape["seq"]),
        mesh=mesh,
        in_specs=in_specs,
        out_specs=out_specs,
        check_vma=False,
    )
```

```python
import functools

import jax
import jax.numpy as jnp
from jax import lax
from jax.experimental import pallas as pl
from jax.experimental.pallas import tpu as pltpu
from jax.sharding import PartitionSpec as P

HEAD_SIZE = 128
HEADS = 16
SPAN = 64
NLEN = 64
READS = 2

NT = (((1,), (1,)), ((), ()))
TN = (((0,), (0,)), ((), ()))
EXTRA = 16
SMALL_BYTES = 4 << 20


def vmem_bytes(rows):
    return (3 << 20) + rows * (13 << 10)


def xor_send(value, axis, size, bit):
    return lax.ppermute(value, axis, [(i, i ^ bit) for i in range(size)])


def bit_reverse(index, bits):
    result = index * 0
    for i in range(bits):
        result = result + (((index >> i) & 1) << (bits - 1 - i))
    return result


def bundles(seq_size, item, dtype):
    sizes = [1] + [1 << b for b in range(seq_size.bit_length() - 1)]
    return [jax.ShapeDtypeStruct((size, *item), dtype) for size in sizes]


def item_of(refs, k):
    return refs[k.bit_length()].at[k - ((1 << k.bit_length()) >> 1)]


def cross(arrays, seq_size, top):
    return [*arrays[:top], xor_send(arrays[top], "seq", seq_size, 1 << (top - 1)), *arrays[top + 1 :]]


def forward(arrays, seq_size):
    top = len(arrays) - 1
    waiting = {b: [(0, array)] for b, array in enumerate(arrays[1:])}
    found = {0: (arrays[0], 0)}
    for b in reversed(range(top)):
        for origin, array in waiting[b]:
            arrived = array if b == top - 1 else xor_send(array, "seq", seq_size, 1 << b)
            origin = origin | (1 << b)
            found[origin] = (arrived, 0)
            for c in range(b):
                waiting[c].append((origin, arrived[1 << c : 2 << c]))
    return [found[j] for j in range(seq_size)]


def exchange(arrays, seq_size):
    return forward(cross(arrays, seq_size, len(arrays) - 1), seq_size)


def operands_of(items):
    arrays = []
    places = []
    for array, index in items:
        at = [array is known for known in arrays]
        if True not in at:
            at.append(True)
            arrays.append(array)
        places.append((at.index(True), index))
    return arrays, places


def pack_body(seq_size, groups, meta, ids, slots, queries, grad_out, *refs):
    held, sems = refs[-2], refs[-1]
    refs = refs[:-2]
    own, first = meta[0], meta[1]
    tokens = queries.shape[1]
    half = tokens // 2
    copies = []
    for part in range(2):
        for which, source in enumerate((queries, grad_out)):
            rows = pl.ds(part * half, half)
            copy = pltpu.make_async_copy(
                source.at[0, rows], held.at[which, rows], sems.at[2 * part + which]
            )
            copy.start()
            copies.append(copy)
    each = len(refs) // len(groups)
    spans = ids.shape[1]
    lanes = lax.broadcasted_iota(jnp.int32, (EXTRA, refs[0].shape[2]), 1)
    positions = jnp.zeros(lanes.shape, jnp.int32)
    for i in range(spans * READS):
        positions = jnp.where(lanes == i, slots[0, ids[0, i // READS, i % READS]], positions)
    positions = positions.astype(jnp.float32).astype(jnp.bfloat16)
    for k in range(seq_size):
        item_of(refs[:each], k)[2 * tokens :, :] = positions
    for part in range(2):
        for which in range(2):
            copies[2 * part + which].wait()
        rows = slice(part * half, (part + 1) * half)
        for g, heads in enumerate(groups):
            arrays = refs[g * each : (g + 1) * each]
            for k in range(seq_size):
                piece = item_of(arrays, k)
                for i, r in enumerate(heads):
                    column = pl.multiple_of(((first ^ r) * seq_size + (own ^ k)) * HEAD_SIZE, HEAD_SIZE)
                    place = slice(i * HEAD_SIZE, (i + 1) * HEAD_SIZE)
                    for which in range(2):
                        target = slice(which * tokens + rows.start, which * tokens + rows.stop)
                        piece[target, place] = held[which, rows, pl.ds(column, HEAD_SIZE)]


def pack(meta, neighbour_ids, slot_map, queries, grad_out, groups, seq_size):
    tokens, columns = queries.shape[1:]
    smem = pl.BlockSpec(memory_space=pltpu.SMEM)
    hbm = pl.BlockSpec(memory_space=pltpu.HBM)
    out_shape = []
    for g, heads in enumerate(groups):
        rows = 2 * tokens + (EXTRA if g == 0 else 0)
        out_shape += bundles(seq_size, (rows, len(heads) * HEAD_SIZE), jnp.bfloat16)
    outs = pl.pallas_call(
        functools.partial(pack_body, seq_size, groups),
        out_shape=out_shape,
        in_specs=[smem] * 3 + [hbm] * 2,
        out_specs=[pl.BlockSpec(memory_space=pltpu.VMEM)] * len(out_shape),
        scratch_shapes=[
            pltpu.VMEM((2, tokens, columns), jnp.bfloat16),
            pltpu.SemaphoreType.DMA((4,)),
        ],
        compiler_params=pltpu.CompilerParams(vmem_limit_bytes=SMALL_BYTES),
        cost_estimate=pl.CostEstimate(flops=0, bytes_accessed=0, transcendentals=0),
        name="pack",
    )(meta, neighbour_ids, slot_map, queries, grad_out)
    each = len(outs) // len(groups)
    return [outs[g * each : (g + 1) * each] for g in range(len(groups))]


def relative_positions(pieces, own, per_owner, tokens):
    bits = len(pieces).bit_length() - 1
    shift = per_owner.bit_length() - 1
    rows = [piece[2 * tokens : 2 * tokens + 8, :HEAD_SIZE] for piece in pieces]
    out = []
    for row in rows:
        position = row.astype(jnp.float32).astype(jnp.int32)
        owner = bit_reverse((position >> shift) ^ own, bits)
        out.append((owner << shift) + (position & (per_owner - 1)))
    return out


def spots_of(table, seq_size, spans):
    spots = []
    for k in range(seq_size):
        for c in range(spans):
            starts = [table[8 * k, c * READS + r] * NLEN for r in range(READS)]
            spots.append((k, c, [pl.multiple_of(start, NLEN) for start in starts]))
    return spots


def attention_body(seq_size, spans, takes, places, arrays, per_owner, finds, has_prior, last, *refs):
    count = len(takes)
    meta, refs = refs[0], refs[1:]
    stored, refs = refs[:seq_size], refs[seq_size:]
    weights, refs = refs[: 2 * count], refs[2 * count :]
    pieces, refs = refs[:arrays], refs[arrays:]
    pieces = [pieces[at].at[index] for at, index in places]
    prior, refs = (refs[0], refs[1:]) if has_prior else (None, refs)
    table, refs = (None, refs) if finds else (refs[0], refs[1:])
    levels = seq_size.bit_length()
    outs, refs = refs[:levels], refs[levels:]
    grads, refs = (refs[:2], refs[2:]) if last else (refs[:1], refs[1:])
    if finds:
        table, refs = refs[0], refs[1:]
    enc, pair, kv, d_kv, found, sem = refs
    block = stored[0].shape[0]
    rows = enc.shape[0]
    tokens = spans * SPAN
    scale = HEAD_SIZE ** (-0.5)
    keys_first = meta[2] == 1
    for i in range(seq_size):
        enc[i * block : (i + 1) * block] = stored[i][...]
    if finds:
        for k, rows_of in enumerate(relative_positions(pieces[:seq_size], meta[0], per_owner, tokens)):
            table[8 * k : 8 * k + 8, :] = rows_of
    copy = pltpu.make_async_copy(table, found, sem)
    copy.start()
    for i in range(count):
        first, second = weights[2 * i][...], weights[2 * i + 1][...]
        pair[:, 2 * i * HEAD_SIZE : (2 * i + 1) * HEAD_SIZE] = jnp.where(keys_first, first, second)
        pair[:, (2 * i + 1) * HEAD_SIZE : (2 * i + 2) * HEAD_SIZE] = jnp.where(keys_first, second, first)
        wide = slice(2 * i * HEAD_SIZE, 2 * (i + 1) * HEAD_SIZE)
        kv[:, wide] = jnp.dot(enc[...], pair[:, wide], preferred_element_type=jnp.float32).astype(jnp.bfloat16)
    d_kv[...] = jnp.zeros_like(d_kv)
    copy.wait()
    units = [(i, *spot) for i in range(count) for spot in spots_of(found, seq_size, spans)]
    reads, queries, grad_rows, scores, d_probs = [], [], [], [], []
    for i, k, c, starts in units:
        wide = slice(2 * i * HEAD_SIZE, 2 * (i + 1) * HEAD_SIZE)
        source, at = takes[i]
        taken = slice(at * HEAD_SIZE, (at + 1) * HEAD_SIZE)
        read = jnp.concatenate([kv[pl.ds(start, NLEN), wide] for start in starts], axis=0)
        query = pieces[source * seq_size + k][c * SPAN : (c + 1) * SPAN, taken]
        grad = pieces[source * seq_size + k][tokens + c * SPAN : tokens + (c + 1) * SPAN, taken]
        reads.append((read[:, :HEAD_SIZE], read[:, HEAD_SIZE:]))
        queries.append(query)
        grad_rows.append(grad)
        scores.append(lax.dot_general(query, reads[-1][0], NT, preferred_element_type=jnp.float32))
        d_probs.append(lax.dot_general(grad, reads[-1][1], NT, preferred_element_type=jnp.float32))
    probs_low, d_scores = [], []
    for score, d_prob in zip(scores, d_probs):
        expos = jnp.exp(score * scale)
        probs = expos * (1.0 / jnp.sum(expos, axis=-1, keepdims=True))
        delta = jnp.sum(probs * d_prob, axis=-1, keepdims=True)
        probs_low.append(probs.astype(jnp.bfloat16))
        d_scores.append((probs * (d_prob - delta) * scale).astype(jnp.bfloat16))
    for n, (i, k, c, _) in enumerate(units):
        keys, values = reads[n]
        span = slice(c * SPAN, (c + 1) * SPAN)
        columns = slice(i * HEAD_SIZE, (i + 1) * HEAD_SIZE)
        item_of(outs, k)[0, span, columns] = jnp.dot(
            probs_low[n], values, preferred_element_type=jnp.float32
        ).astype(jnp.bfloat16)
        item_of(outs, k)[1, span, columns] = jnp.dot(
            d_scores[n], keys, preferred_element_type=jnp.float32
        ).astype(jnp.bfloat16)
    both = [
        (
            lax.dot_general(d_scores[n], queries[n], TN, preferred_element_type=jnp.float32),
            lax.dot_general(probs_low[n], grad_rows[n], TN, preferred_element_type=jnp.float32),
        )
        for n in range(len(units))
    ]
    for n, (i, _, _, starts) in enumerate(units):
        for r, start in enumerate(starts):
            for part in range(2):
                wide = slice((2 * i + part) * HEAD_SIZE, (2 * i + part + 1) * HEAD_SIZE)
                d_kv[pl.ds(start, NLEN), wide] += both[n][part][r * NLEN : (r + 1) * NLEN]
    half = rows // 2
    for part in range(2):
        place = slice(part * half, (part + 1) * half)
        term = lax.dot_general(
            d_kv[place, :].astype(jnp.bfloat16), pair[...], NT, preferred_element_type=jnp.float32
        )
        if has_prior:
            term = term + prior[place, :].astype(jnp.float32)
        if last:
            grads[part][...] = term.astype(grads[part].dtype)
        else:
            grads[0][place, :] = term.astype(grads[0].dtype)


def attention(meta, table, stored, weights, takes, spans, per_owner, prior, last):
    seq_size = len(stored)
    sources = []
    for source, _ in takes:
        if not any(source is known for known in sources):
            sources.append(source)
    takes = [([source is known for known in sources].index(True), at) for source, at in takes]
    arrays, places = operands_of([item for source in sources for item in source])
    block, width = stored[0].shape
    rows = seq_size * block
    count = len(weights) // 2
    prior = [] if prior is None else [prior]
    vmem = pl.BlockSpec(memory_space=pltpu.VMEM)
    finds = table is None
    operands = [*stored, *weights, *arrays, *prior] + ([] if finds else [table])
    table_shape = (8 * seq_size, HEAD_SIZE)
    out_shape = bundles(seq_size, (2, spans * SPAN, count * HEAD_SIZE), jnp.bfloat16)
    levels = len(out_shape)
    if last:
        out_shape.append(jax.ShapeDtypeStruct((rows // 2, width), jnp.float32))
        out_shape.append(jax.ShapeDtypeStruct((rows // 2, width), jnp.bfloat16))
    else:
        out_shape.append(jax.ShapeDtypeStruct((rows, width), jnp.bfloat16))
    grads = len(out_shape) - levels
    scratch = [
        pltpu.VMEM((rows, width), jnp.bfloat16),
        pltpu.VMEM((width, 2 * count * HEAD_SIZE), jnp.bfloat16),
        pltpu.VMEM((rows, 2 * count * HEAD_SIZE), jnp.bfloat16),
        pltpu.VMEM((rows, 2 * count * HEAD_SIZE), jnp.float32),
        pltpu.SMEM(table_shape, jnp.int32),
        pltpu.SemaphoreType.DMA,
    ]
    if finds:
        out_shape.append(jax.ShapeDtypeStruct(table_shape, jnp.int32))
    outs = pl.pallas_call(
        functools.partial(
            attention_body, seq_size, spans, takes, places, len(arrays), per_owner, finds, len(prior), last
        ),
        out_shape=out_shape,
        in_specs=[pl.BlockSpec(memory_space=pltpu.SMEM)] + [vmem] * len(operands),
        out_specs=[vmem] * len(out_shape),
        scratch_shapes=scratch,
        compiler_params=pltpu.CompilerParams(vmem_limit_bytes=vmem_bytes(rows)),
        cost_estimate=pl.CostEstimate(
            flops=int(2.4e9) if last and len(prior) else 0, bytes_accessed=0, transcendentals=0
        ),
        name="attention",
    )(meta, *operands)
    return outs[:levels], outs[levels : levels + grads], outs[-1] if finds else table


def unpack_body(seq_size, groups, places, meta, *refs):
    attended, grad_queries = refs[-2:]
    own, first = meta[0], meta[1]
    for g, heads in enumerate(groups):
        for k in range(seq_size):
            at, index = places[g * seq_size + k]
            for i, r in enumerate(heads):
                column = pl.multiple_of(((first ^ r) * seq_size + (own ^ k)) * HEAD_SIZE, HEAD_SIZE)
                place = slice(i * HEAD_SIZE, (i + 1) * HEAD_SIZE)
                attended[0, :, pl.ds(column, HEAD_SIZE)] = refs[at][index, 0, :, place]
                grad_queries[0, :, pl.ds(column, HEAD_SIZE)] = refs[at][index, 1, :, place]


def unpack(meta, items, groups, seq_size):
    arrays, places = operands_of(items)
    tokens = arrays[0].shape[2]
    shape = jax.ShapeDtypeStruct((1, tokens, HEADS * HEAD_SIZE), jnp.bfloat16)
    vmem = pl.BlockSpec(memory_space=pltpu.VMEM)
    return pl.pallas_call(
        functools.partial(unpack_body, seq_size, groups, places),
        out_shape=[shape, shape],
        in_specs=[pl.BlockSpec(memory_space=pltpu.SMEM)] + [vmem] * len(arrays),
        out_specs=[vmem, vmem],
        compiler_params=pltpu.CompilerParams(vmem_limit_bytes=SMALL_BYTES),
        cost_estimate=pl.CostEstimate(flops=0, bytes_accessed=0, transcendentals=0),
        name="unpack",
    )(meta, *arrays)


def weight_slice(kv_weight, column):
    return lax.dynamic_slice_in_dim(kv_weight, column, HEAD_SIZE, axis=1)


def whole_weights(kv_weight, own, seq_size):
    whole = lax.all_gather(kv_weight, "dp", axis=1, tiled=True)
    pairs = []
    for r in range(HEADS // seq_size):
        column = (r * seq_size + own) * HEAD_SIZE
        pairs.append((weight_slice(whole, column), weight_slice(whole, column + HEADS * HEAD_SIZE)))
    return pairs


def tie(*values):
    return lax.optimization_barrier(values)


def fold(total, arrived):
    total = total + arrived.astype(jnp.float32)
    half = total.shape[0] // 2
    return total[:half], total[half:].astype(jnp.bfloat16)


def tie_items(value, items):
    tied = lax.optimization_barrier((value, [array for array, _ in items]))
    return tied[0], [(array, index) for array, (_, index) in zip(tied[1], items)]


def per_device(dp_size, seq_size, queries, grad_out, encoded, kv_weight, neighbour_ids, slot_map):
    own = lax.axis_index("seq")
    place = lax.axis_index("dp")
    bits = seq_size.bit_length() - 1
    per_owner = encoded.shape[1]
    spans = neighbour_ids.shape[1]
    tokens = queries.shape[1]
    width = encoded.shape[3]
    pool_size = slot_map.shape[1]
    assert pool_size <= 256 and 1 << bits == seq_size and per_owner & (per_owner - 1) == 0
    split = dp_size == 8 and 2 * HEADS == dp_size * seq_size
    send = functools.partial(xor_send, axis="seq", size=seq_size)
    move = functools.partial(xor_send, axis="dp", size=dp_size)

    if split:
        first = place % (HEADS // seq_size)
        keys_first = (place < dp_size // 2).astype(jnp.int32)
        groups = [(0,), (1, 2), (3,)]
        packed = [(0,), (1, 2, 3)]
    else:
        first, keys_first = place * 0, place * 0 + 1
        groups = packed = [tuple(range(HEADS // seq_size))]

    head_meta = jnp.stack([own, first, keys_first, place])
    pieces = pack(head_meta, neighbour_ids, slot_map, queries, grad_out, packed, seq_size)
    stored = [encoded[0].reshape(per_owner * NLEN, width)]
    if not split:
        for level in range(bits - 1, -1, -1):
            stored = stored + [send(rows, bit=1 << level) for rows in stored]
    if split:
        mine = weight_slice(kv_weight, own * HEAD_SIZE)
        stored = stored + [send(stored[0], bit=2)]
        stored = stored + [send(rows, bit=1) for rows in stored]
        early = cross(pieces[0], seq_size, bits)
        far, near, side, late = tie(move(mine, bit=4), move(mine, bit=2), move(mine, bit=1), pieces[1])
        near_far = move(far, bit=2)
        side_far = move(far, bit=1)
        early = forward(early, seq_size)
        late = cross(late, seq_size, bits)
        attend = functools.partial(attention, head_meta, spans=spans, per_owner=per_owner)
        outs, (grads,), table = attend(
            None, stored, [mine, far], [(early, 0)], prior=None, last=False
        )
        near_far, outs = tie(near_far, outs)
        parts_a = cross(outs, seq_size, bits)
        near_far, side_far, side, near, late, grads = tie(near_far, side_far, side, near, late, grads)
        side_near_far, side_near = move(near_far, bit=1), move(side, bit=2)
        late = forward(late, seq_size)
        outs, (grads,), _ = attend(
            table, stored, [side, side_far, near, near_far], [(late, 0), (late, 1)], prior=grads, last=False
        )
        parts_b = cross(outs, seq_size, bits)
        grads, parts_a = tie(grads, parts_a)
        outs, grads, _ = attend(
            table, stored, [side_near, side_near_far], [(late, 2)], prior=grads, last=True
        )
        parts_c = cross(outs, seq_size, bits)
        grads, parts_b = tie(grads, parts_b)
        total, leaving = fold(grads[0], send(grads[1], bit=1))
        items = [item for parts in (parts_a, parts_b, parts_c) for item in forward(parts, seq_size)]
    else:
        weights = [block for pair in whole_weights(kv_weight, own, seq_size) for block in pair]
        early = exchange(pieces[0], seq_size)
        takes = [(early, i) for i in range(HEADS // seq_size)]
        outs, grads, _ = attention(head_meta, None, stored, weights, takes, spans, per_owner, None, True)
        items = exchange(outs, seq_size)
    if not split:
        total, leaving = grads
        for level in range(bits - 1):
            total, leaving = fold(total, send(leaving, bit=1 << level))
    total = total + send(leaving, bit=1 << (bits - 1)).astype(jnp.float32)
    attended, grad_queries = unpack(head_meta, items, groups, seq_size)
    return attended, grad_queries, total.reshape(1, per_owner, NLEN, width)


def solution(mesh):
    in_specs = (
        P("dp", "seq", None),
        P("dp", "seq", None),
        P("dp", "seq", None, None),
        P(None, "dp"),
        P("dp", "seq", None),
        P("dp", None),
    )
    out_specs = (P("dp", "seq", None), P("dp", "seq", None), P("dp", "seq", None, None))
    return jax.shard_map(
        functools.partial(per_device, mesh.shape["dp"], mesh.shape["seq"]),
        mesh=mesh,
        in_specs=in_specs,
        out_specs=out_specs,
        check_vma=False,
    )
```

```python
import functools

import jax
import jax.numpy as jnp
from jax import lax
from jax.experimental import pallas as pl
from jax.experimental.pallas import tpu as pltpu
from jax.sharding import PartitionSpec as P

HEAD_SIZE = 128
HEADS = 16
SPAN = 64
NLEN = 64
READS = 2

NT = (((1,), (1,)), ((), ()))
TN = (((0,), (0,)), ((), ()))
EXTRA = 16
SMALL_BYTES = 4 << 20


def vmem_bytes(rows):
    return (3 << 20) + rows * (13 << 10)


def xor_send(value, axis, size, bit):
    return lax.ppermute(value, axis, [(i, i ^ bit) for i in range(size)])


def bit_reverse(index, bits):
    result = index * 0
    for i in range(bits):
        result = result + (((index >> i) & 1) << (bits - 1 - i))
    return result


def bundles(seq_size, item, dtype):
    sizes = [1] + [1 << b for b in range(seq_size.bit_length() - 1)]
    return [jax.ShapeDtypeStruct((size, *item), dtype) for size in sizes]


def item_of(refs, k):
    return refs[k.bit_length()].at[k - ((1 << k.bit_length()) >> 1)]


def cross(arrays, seq_size, top):
    return [*arrays[:top], xor_send(arrays[top], "seq", seq_size, 1 << (top - 1)), *arrays[top + 1 :]]


def forward(arrays, seq_size):
    top = len(arrays) - 1
    waiting = {b: [(0, array)] for b, array in enumerate(arrays[1:])}
    found = {0: (arrays[0], 0)}
    for b in reversed(range(top)):
        for origin, array in waiting[b]:
            arrived = array if b == top - 1 else xor_send(array, "seq", seq_size, 1 << b)
            origin = origin | (1 << b)
            found[origin] = (arrived, 0)
            for c in range(b):
                waiting[c].append((origin, arrived[1 << c : 2 << c]))
    return [found[j] for j in range(seq_size)]


def exchange(arrays, seq_size):
    return forward(cross(arrays, seq_size, len(arrays) - 1), seq_size)


def operands_of(items):
    arrays = []
    places = []
    for array, index in items:
        at = [array is known for known in arrays]
        if True not in at:
            at.append(True)
            arrays.append(array)
        places.append((at.index(True), index))
    return arrays, places


def pack_body(seq_size, groups, meta, ids, slots, queries, grad_out, *refs):
    held, sems = refs[-2], refs[-1]
    refs = refs[:-2]
    own, first = meta[0], meta[1]
    tokens = queries.shape[1]
    half = tokens // 2
    copies = []
    for part in range(2):
        for which, source in enumerate((queries, grad_out)):
            rows = pl.ds(part * half, half)
            copy = pltpu.make_async_copy(
                source.at[0, rows], held.at[which, rows], sems.at[2 * part + which]
            )
            copy.start()
            copies.append(copy)
    each = len(refs) // len(groups)
    spans = ids.shape[1]
    lanes = lax.broadcasted_iota(jnp.int32, (EXTRA, refs[0].shape[2]), 1)
    positions = jnp.zeros(lanes.shape, jnp.int32)
    for i in range(spans * READS):
        positions = jnp.where(lanes == i, slots[0, ids[0, i // READS, i % READS]], positions)
    positions = positions.astype(jnp.float32).astype(jnp.bfloat16)
    for k in range(seq_size):
        item_of(refs[:each], k)[2 * tokens :, :] = positions
    for part in range(2):
        for which in range(2):
            copies[2 * part + which].wait()
        rows = slice(part * half, (part + 1) * half)
        for g, heads in enumerate(groups):
            arrays = refs[g * each : (g + 1) * each]
            for k in range(seq_size):
                piece = item_of(arrays, k)
                for i, r in enumerate(heads):
                    column = pl.multiple_of(((first ^ r) * seq_size + (own ^ k)) * HEAD_SIZE, HEAD_SIZE)
                    place = slice(i * HEAD_SIZE, (i + 1) * HEAD_SIZE)
                    for which in range(2):
                        target = slice(which * tokens + rows.start, which * tokens + rows.stop)
                        piece[target, place] = held[which, rows, pl.ds(column, HEAD_SIZE)]


def pack(meta, neighbour_ids, slot_map, queries, grad_out, groups, seq_size):
    tokens, columns = queries.shape[1:]
    smem = pl.BlockSpec(memory_space=pltpu.SMEM)
    hbm = pl.BlockSpec(memory_space=pltpu.HBM)
    out_shape = []
    for g, heads in enumerate(groups):
        rows = 2 * tokens + (EXTRA if g == 0 else 0)
        out_shape += bundles(seq_size, (rows, len(heads) * HEAD_SIZE), jnp.bfloat16)
    outs = pl.pallas_call(
        functools.partial(pack_body, seq_size, groups),
        out_shape=out_shape,
        in_specs=[smem] * 3 + [hbm] * 2,
        out_specs=[pl.BlockSpec(memory_space=pltpu.VMEM)] * len(out_shape),
        scratch_shapes=[
            pltpu.VMEM((2, tokens, columns), jnp.bfloat16),
            pltpu.SemaphoreType.DMA((4,)),
        ],
        compiler_params=pltpu.CompilerParams(vmem_limit_bytes=SMALL_BYTES),
        cost_estimate=pl.CostEstimate(flops=0, bytes_accessed=0, transcendentals=0),
        name="pack",
    )(meta, neighbour_ids, slot_map, queries, grad_out)
    each = len(outs) // len(groups)
    return [outs[g * each : (g + 1) * each] for g in range(len(groups))]


def relative_positions(pieces, own, per_owner, tokens):
    bits = len(pieces).bit_length() - 1
    shift = per_owner.bit_length() - 1
    rows = [piece[2 * tokens : 2 * tokens + 8, :HEAD_SIZE] for piece in pieces]
    out = []
    for row in rows:
        position = row.astype(jnp.float32).astype(jnp.int32)
        owner = bit_reverse((position >> shift) ^ own, bits)
        out.append((owner << shift) + (position & (per_owner - 1)))
    return out


def spots_of(table, seq_size, spans):
    spots = []
    for k in range(seq_size):
        for c in range(spans):
            starts = [table[8 * k, c * READS + r] * NLEN for r in range(READS)]
            spots.append((k, c, [pl.multiple_of(start, NLEN) for start in starts]))
    return spots


def attention_body(seq_size, spans, takes, places, arrays, per_owner, finds, has_prior, last, *refs):
    count = len(takes)
    meta, refs = refs[0], refs[1:]
    stored, refs = refs[:seq_size], refs[seq_size:]
    weights, refs = refs[: 2 * count], refs[2 * count :]
    pieces, refs = refs[:arrays], refs[arrays:]
    pieces = [pieces[at].at[index] for at, index in places]
    prior, refs = (refs[0], refs[1:]) if has_prior else (None, refs)
    table, refs = (None, refs) if finds else (refs[0], refs[1:])
    levels = seq_size.bit_length()
    outs, refs = refs[:levels], refs[levels:]
    grads, refs = (refs[:2], refs[2:]) if last else (refs[:1], refs[1:])
    if finds:
        table, refs = refs[0], refs[1:]
    pair, kv, d_kv, found, sem = refs
    block = stored[0].shape[0]
    rows = d_kv.shape[0]
    tokens = spans * SPAN
    scale = HEAD_SIZE ** (-0.5)
    keys_first = meta[2] == 1
    if finds:
        for k, rows_of in enumerate(relative_positions(pieces[:seq_size], meta[0], per_owner, tokens)):
            table[8 * k : 8 * k + 8, :] = rows_of
    copy = pltpu.make_async_copy(table, found, sem)
    copy.start()
    for i in range(count):
        first, second = weights[2 * i][...], weights[2 * i + 1][...]
        pair[:, 2 * i * HEAD_SIZE : (2 * i + 1) * HEAD_SIZE] = jnp.where(keys_first, first, second)
        pair[:, (2 * i + 1) * HEAD_SIZE : (2 * i + 2) * HEAD_SIZE] = jnp.where(keys_first, second, first)
        wide = slice(2 * i * HEAD_SIZE, 2 * (i + 1) * HEAD_SIZE)
        for n in range(seq_size):
            kv[n * block : (n + 1) * block, wide] = jnp.dot(
                stored[n][...], pair[:, wide], preferred_element_type=jnp.float32
            ).astype(jnp.bfloat16)
    d_kv[...] = jnp.zeros_like(d_kv)
    copy.wait()
    units = [(i, *spot) for i in range(count) for spot in spots_of(found, seq_size, spans)]
    reads, queries, grad_rows, scores, d_probs = [], [], [], [], []
    for i, k, c, starts in units:
        wide = slice(2 * i * HEAD_SIZE, 2 * (i + 1) * HEAD_SIZE)
        source, at = takes[i]
        taken = slice(at * HEAD_SIZE, (at + 1) * HEAD_SIZE)
        read = jnp.concatenate([kv[pl.ds(start, NLEN), wide] for start in starts], axis=0)
        query = pieces[source * seq_size + k][c * SPAN : (c + 1) * SPAN, taken]
        grad = pieces[source * seq_size + k][tokens + c * SPAN : tokens + (c + 1) * SPAN, taken]
        reads.append((read[:, :HEAD_SIZE], read[:, HEAD_SIZE:]))
        queries.append(query)
        grad_rows.append(grad)
        scores.append(lax.dot_general(query, reads[-1][0], NT, preferred_element_type=jnp.float32))
        d_probs.append(lax.dot_general(grad, reads[-1][1], NT, preferred_element_type=jnp.float32))
    probs_low, d_scores = [], []
    for score, d_prob in zip(scores, d_probs):
        expos = jnp.exp(score * scale)
        probs = expos * (1.0 / jnp.sum(expos, axis=-1, keepdims=True))
        delta = jnp.sum(probs * d_prob, axis=-1, keepdims=True)
        probs_low.append(probs.astype(jnp.bfloat16))
        d_scores.append((probs * (d_prob - delta) * scale).astype(jnp.bfloat16))
    for n, (i, k, c, _) in enumerate(units):
        keys, values = reads[n]
        span = slice(c * SPAN, (c + 1) * SPAN)
        columns = slice(i * HEAD_SIZE, (i + 1) * HEAD_SIZE)
        item_of(outs, k)[0, span, columns] = jnp.dot(
            probs_low[n], values, preferred_element_type=jnp.float32
        ).astype(jnp.bfloat16)
        item_of(outs, k)[1, span, columns] = jnp.dot(
            d_scores[n], keys, preferred_element_type=jnp.float32
        ).astype(jnp.bfloat16)
    both = [
        (
            lax.dot_general(d_scores[n], queries[n], TN, preferred_element_type=jnp.float32),
            lax.dot_general(probs_low[n], grad_rows[n], TN, preferred_element_type=jnp.float32),
        )
        for n in range(len(units))
    ]
    for n, (i, _, _, starts) in enumerate(units):
        for r, start in enumerate(starts):
            for part in range(2):
                wide = slice((2 * i + part) * HEAD_SIZE, (2 * i + part + 1) * HEAD_SIZE)
                d_kv[pl.ds(start, NLEN), wide] += both[n][part][r * NLEN : (r + 1) * NLEN]
    half = rows // 2
    for part in range(2):
        place = slice(part * half, (part + 1) * half)
        term = lax.dot_general(
            d_kv[place, :].astype(jnp.bfloat16), pair[...], NT, preferred_element_type=jnp.float32
        )
        if has_prior:
            term = term + prior[place, :].astype(jnp.float32)
        if last:
            grads[part][...] = term.astype(grads[part].dtype)
        else:
            grads[0][place, :] = term.astype(grads[0].dtype)


def attention(meta, table, stored, weights, takes, spans, per_owner, prior, last):
    seq_size = len(stored)
    sources = []
    for source, _ in takes:
        if not any(source is known for known in sources):
            sources.append(source)
    takes = [([source is known for known in sources].index(True), at) for source, at in takes]
    arrays, places = operands_of([item for source in sources for item in source])
    block, width = stored[0].shape
    rows = seq_size * block
    count = len(weights) // 2
    prior = [] if prior is None else [prior]
    vmem = pl.BlockSpec(memory_space=pltpu.VMEM)
    finds = table is None
    operands = [*stored, *weights, *arrays, *prior] + ([] if finds else [table])
    table_shape = (8 * seq_size, HEAD_SIZE)
    out_shape = bundles(seq_size, (2, spans * SPAN, count * HEAD_SIZE), jnp.bfloat16)
    levels = len(out_shape)
    if last:
        out_shape.append(jax.ShapeDtypeStruct((rows // 2, width), jnp.float32))
        out_shape.append(jax.ShapeDtypeStruct((rows // 2, width), jnp.bfloat16))
    else:
        out_shape.append(jax.ShapeDtypeStruct((rows, width), jnp.bfloat16))
    grads = len(out_shape) - levels
    scratch = [
        pltpu.VMEM((width, 2 * count * HEAD_SIZE), jnp.bfloat16),
        pltpu.VMEM((rows, 2 * count * HEAD_SIZE), jnp.bfloat16),
        pltpu.VMEM((rows, 2 * count * HEAD_SIZE), jnp.float32),
        pltpu.SMEM(table_shape, jnp.int32),
        pltpu.SemaphoreType.DMA,
    ]
    if finds:
        out_shape.append(jax.ShapeDtypeStruct(table_shape, jnp.int32))
    outs = pl.pallas_call(
        functools.partial(
            attention_body, seq_size, spans, takes, places, len(arrays), per_owner, finds, len(prior), last
        ),
        out_shape=out_shape,
        in_specs=[pl.BlockSpec(memory_space=pltpu.SMEM)] + [vmem] * len(operands),
        out_specs=[vmem] * len(out_shape),
        scratch_shapes=scratch,
        compiler_params=pltpu.CompilerParams(vmem_limit_bytes=vmem_bytes(rows)),
        cost_estimate=pl.CostEstimate(
            flops=int(2.4e9) if last and len(prior) else 0, bytes_accessed=0, transcendentals=0
        ),
        name="attention",
    )(meta, *operands)
    return outs[:levels], outs[levels : levels + grads], outs[-1] if finds else table


def unpack_body(seq_size, groups, places, meta, *refs):
    attended, grad_queries = refs[-2:]
    own, first = meta[0], meta[1]
    for g, heads in enumerate(groups):
        for k in range(seq_size):
            at, index = places[g * seq_size + k]
            for i, r in enumerate(heads):
                column = pl.multiple_of(((first ^ r) * seq_size + (own ^ k)) * HEAD_SIZE, HEAD_SIZE)
                place = slice(i * HEAD_SIZE, (i + 1) * HEAD_SIZE)
                attended[0, :, pl.ds(column, HEAD_SIZE)] = refs[at][index, 0, :, place]
                grad_queries[0, :, pl.ds(column, HEAD_SIZE)] = refs[at][index, 1, :, place]


def unpack(meta, items, groups, seq_size):
    arrays, places = operands_of(items)
    tokens = arrays[0].shape[2]
    shape = jax.ShapeDtypeStruct((1, tokens, HEADS * HEAD_SIZE), jnp.bfloat16)
    vmem = pl.BlockSpec(memory_space=pltpu.VMEM)
    return pl.pallas_call(
        functools.partial(unpack_body, seq_size, groups, places),
        out_shape=[shape, shape],
        in_specs=[pl.BlockSpec(memory_space=pltpu.SMEM)] + [vmem] * len(arrays),
        out_specs=[vmem, vmem],
        compiler_params=pltpu.CompilerParams(vmem_limit_bytes=SMALL_BYTES),
        cost_estimate=pl.CostEstimate(flops=0, bytes_accessed=0, transcendentals=0),
        name="unpack",
    )(meta, *arrays)


def weight_slice(kv_weight, column):
    return lax.dynamic_slice_in_dim(kv_weight, column, HEAD_SIZE, axis=1)


def whole_weights(kv_weight, own, seq_size):
    whole = lax.all_gather(kv_weight, "dp", axis=1, tiled=True)
    pairs = []
    for r in range(HEADS // seq_size):
        column = (r * seq_size + own) * HEAD_SIZE
        pairs.append((weight_slice(whole, column), weight_slice(whole, column + HEADS * HEAD_SIZE)))
    return pairs


def tie(*values):
    return lax.optimization_barrier(values)


def fold(total, arrived):
    total = total + arrived.astype(jnp.float32)
    half = total.shape[0] // 2
    return total[:half], total[half:].astype(jnp.bfloat16)


def tie_items(value, items):
    tied = lax.optimization_barrier((value, [array for array, _ in items]))
    return tied[0], [(array, index) for array, (_, index) in zip(tied[1], items)]


def per_device(dp_size, seq_size, queries, grad_out, encoded, kv_weight, neighbour_ids, slot_map):
    own = lax.axis_index("seq")
    place = lax.axis_index("dp")
    bits = seq_size.bit_length() - 1
    per_owner = encoded.shape[1]
    spans = neighbour_ids.shape[1]
    tokens = queries.shape[1]
    width = encoded.shape[3]
    pool_size = slot_map.shape[1]
    assert pool_size <= 256 and 1 << bits == seq_size and per_owner & (per_owner - 1) == 0
    split = dp_size == 8 and 2 * HEADS == dp_size * seq_size
    send = functools.partial(xor_send, axis="seq", size=seq_size)
    move = functools.partial(xor_send, axis="dp", size=dp_size)

    if split:
        first = place % (HEADS // seq_size)
        keys_first = (place < dp_size // 2).astype(jnp.int32)
        groups = [(0,), (1, 2), (3,)]
        packed = [(0,), (1, 2, 3)]
    else:
        first, keys_first = place * 0, place * 0 + 1
        groups = packed = [tuple(range(HEADS // seq_size))]

    head_meta = jnp.stack([own, first, keys_first, place])
    pieces = pack(head_meta, neighbour_ids, slot_map, queries, grad_out, packed, seq_size)
    stored = [encoded[0].reshape(per_owner * NLEN, width)]
    if not split:
        for level in range(bits - 1, -1, -1):
            stored = stored + [send(rows, bit=1 << level) for rows in stored]
    if split:
        mine = weight_slice(kv_weight, own * HEAD_SIZE)
        stored = stored + [send(stored[0], bit=2)]
        stored = stored + [send(rows, bit=1) for rows in stored]
        early = cross(pieces[0], seq_size, bits)
        far, near, side, late = tie(move(mine, bit=4), move(mine, bit=2), move(mine, bit=1), pieces[1])
        near_far = move(far, bit=2)
        side_far = move(far, bit=1)
        early = forward(early, seq_size)
        late = cross(late, seq_size, bits)
        attend = functools.partial(attention, head_meta, spans=spans, per_owner=per_owner)
        outs, (grads,), table = attend(
            None, stored, [mine, far], [(early, 0)], prior=None, last=False
        )
        near_far, outs = tie(near_far, outs)
        parts_a = cross(outs, seq_size, bits)
        near_far, side_far, side, near, late, grads = tie(near_far, side_far, side, near, late, grads)
        side_near_far, side_near = move(near_far, bit=1), move(side, bit=2)
        late = forward(late, seq_size)
        outs, (grads,), _ = attend(
            table, stored, [side, side_far, near, near_far], [(late, 0), (late, 1)], prior=grads, last=False
        )
        parts_b = cross(outs, seq_size, bits)
        grads, parts_a = tie(grads, parts_a)
        outs, grads, _ = attend(
            table, stored, [side_near, side_near_far], [(late, 2)], prior=grads, last=True
        )
        parts_c = cross(outs, seq_size, bits)
        grads, parts_b = tie(grads, parts_b)
        total, leaving = fold(grads[0], send(grads[1], bit=1))
        items = [item for parts in (parts_a, parts_b, parts_c) for item in forward(parts, seq_size)]
    else:
        weights = [block for pair in whole_weights(kv_weight, own, seq_size) for block in pair]
        early = exchange(pieces[0], seq_size)
        takes = [(early, i) for i in range(HEADS // seq_size)]
        outs, grads, _ = attention(head_meta, None, stored, weights, takes, spans, per_owner, None, True)
        items = exchange(outs, seq_size)
    if not split:
        total, leaving = grads
        for level in range(bits - 1):
            total, leaving = fold(total, send(leaving, bit=1 << level))
    total = total + send(leaving, bit=1 << (bits - 1)).astype(jnp.float32)
    attended, grad_queries = unpack(head_meta, items, groups, seq_size)
    return attended, grad_queries, total.reshape(1, per_owner, NLEN, width)


def solution(mesh):
    in_specs = (
        P("dp", "seq", None),
        P("dp", "seq", None),
        P("dp", "seq", None, None),
        P(None, "dp"),
        P("dp", "seq", None),
        P("dp", None),
    )
    out_specs = (P("dp", "seq", None), P("dp", "seq", None), P("dp", "seq", None, None))
    return jax.shard_map(
        functools.partial(per_device, mesh.shape["dp"], mesh.shape["seq"]),
        mesh=mesh,
        in_specs=in_specs,
        out_specs=out_specs,
        check_vma=False,
    )
```

```python
import functools

import jax
import jax.numpy as jnp
from jax import lax
from jax.experimental import pallas as pl
from jax.experimental.pallas import tpu as pltpu
from jax.sharding import PartitionSpec as P

HEAD_SIZE = 128
HEADS = 16
SPAN = 64
NLEN = 64
READS = 2

NT = (((1,), (1,)), ((), ()))
TN = (((0,), (0,)), ((), ()))
EXTRA = 16
SMALL_BYTES = 4 << 20


def vmem_bytes(rows):
    return (3 << 20) + rows * (13 << 10)


def xor_send(value, axis, size, bit):
    return lax.ppermute(value, axis, [(i, i ^ bit) for i in range(size)])


def bit_reverse(index, bits):
    result = index * 0
    for i in range(bits):
        result = result + (((index >> i) & 1) << (bits - 1 - i))
    return result


def bundles(seq_size, item, dtype):
    sizes = [1] + [1 << b for b in range(seq_size.bit_length() - 1)]
    return [jax.ShapeDtypeStruct((size, *item), dtype) for size in sizes]


def item_of(refs, k):
    return refs[k.bit_length()].at[k - ((1 << k.bit_length()) >> 1)]


def cross(arrays, seq_size, top):
    return [*arrays[:top], xor_send(arrays[top], "seq", seq_size, 1 << (top - 1)), *arrays[top + 1 :]]


def forward(arrays, seq_size):
    top = len(arrays) - 1
    waiting = {b: [(0, array)] for b, array in enumerate(arrays[1:])}
    found = {0: (arrays[0], 0)}
    for b in reversed(range(top)):
        for origin, array in waiting[b]:
            arrived = array if b == top - 1 else xor_send(array, "seq", seq_size, 1 << b)
            origin = origin | (1 << b)
            found[origin] = (arrived, 0)
            for c in range(b):
                waiting[c].append((origin, arrived[1 << c : 2 << c]))
    return [found[j] for j in range(seq_size)]


def exchange(arrays, seq_size):
    return forward(cross(arrays, seq_size, len(arrays) - 1), seq_size)


def operands_of(items):
    arrays = []
    places = []
    for array, index in items:
        at = [array is known for known in arrays]
        if True not in at:
            at.append(True)
            arrays.append(array)
        places.append((at.index(True), index))
    return arrays, places


def pack_body(seq_size, groups, meta, ids, slots, queries, grad_out, *refs):
    held, sems = refs[-2], refs[-1]
    refs = refs[:-2]
    own, first = meta[0], meta[1]
    tokens = queries.shape[1]
    half = tokens // 2
    copies = []
    for part in range(2):
        for which, source in enumerate((queries, grad_out)):
            rows = pl.ds(part * half, half)
            copy = pltpu.make_async_copy(
                source.at[0, rows], held.at[which, rows], sems.at[2 * part + which]
            )
            copy.start()
            copies.append(copy)
    each = len(refs) // len(groups)
    spans = ids.shape[1]
    lanes = lax.broadcasted_iota(jnp.int32, (EXTRA, refs[0].shape[2]), 1)
    positions = jnp.zeros(lanes.shape, jnp.int32)
    for i in range(spans * READS):
        positions = jnp.where(lanes == i, slots[0, ids[0, i // READS, i % READS]], positions)
    positions = positions.astype(jnp.float32).astype(jnp.bfloat16)
    for k in range(seq_size):
        item_of(refs[:each], k)[2 * tokens :, :] = positions
    for part in range(2):
        for which in range(2):
            copies[2 * part + which].wait()
        rows = slice(part * half, (part + 1) * half)
        for g, heads in enumerate(groups):
            arrays = refs[g * each : (g + 1) * each]
            for k in range(seq_size):
                piece = item_of(arrays, k)
                for i, r in enumerate(heads):
                    column = pl.multiple_of(((first ^ r) * seq_size + (own ^ k)) * HEAD_SIZE, HEAD_SIZE)
                    place = slice(i * HEAD_SIZE, (i + 1) * HEAD_SIZE)
                    for which in range(2):
                        target = slice(which * tokens + rows.start, which * tokens + rows.stop)
                        piece[target, place] = held[which, rows, pl.ds(column, HEAD_SIZE)]


def pack(meta, neighbour_ids, slot_map, queries, grad_out, groups, seq_size):
    tokens, columns = queries.shape[1:]
    smem = pl.BlockSpec(memory_space=pltpu.SMEM)
    hbm = pl.BlockSpec(memory_space=pltpu.HBM)
    out_shape = []
    for g, heads in enumerate(groups):
        rows = 2 * tokens + (EXTRA if g == 0 else 0)
        out_shape += bundles(seq_size, (rows, len(heads) * HEAD_SIZE), jnp.bfloat16)
    outs = pl.pallas_call(
        functools.partial(pack_body, seq_size, groups),
        out_shape=out_shape,
        in_specs=[smem] * 3 + [hbm] * 2,
        out_specs=[pl.BlockSpec(memory_space=pltpu.VMEM)] * len(out_shape),
        scratch_shapes=[
            pltpu.VMEM((2, tokens, columns), jnp.bfloat16),
            pltpu.SemaphoreType.DMA((4,)),
        ],
        compiler_params=pltpu.CompilerParams(vmem_limit_bytes=SMALL_BYTES),
        cost_estimate=pl.CostEstimate(flops=0, bytes_accessed=0, transcendentals=0),
        name="pack",
    )(meta, neighbour_ids, slot_map, queries, grad_out)
    each = len(outs) // len(groups)
    return [outs[g * each : (g + 1) * each] for g in range(len(groups))]


def relative_positions(pieces, own, per_owner, tokens):
    bits = len(pieces).bit_length() - 1
    shift = per_owner.bit_length() - 1
    rows = [piece[2 * tokens : 2 * tokens + EXTRA, :HEAD_SIZE] for piece in pieces]
    out = []
    for row in rows:
        position = row.astype(jnp.float32).astype(jnp.int32)[:8]
        owner = bit_reverse((position >> shift) ^ own, bits)
        out.append((owner << shift) + (position & (per_owner - 1)))
    return out


def spots_of(table, seq_size, spans):
    spots = []
    for k in range(seq_size):
        for c in range(spans):
            starts = [table[8 * k, c * READS + r] * NLEN for r in range(READS)]
            spots.append((k, c, [pl.multiple_of(start, NLEN) for start in starts]))
    return spots


def attention_body(seq_size, spans, takes, places, arrays, per_owner, finds, has_prior, last, *refs):
    count = len(takes)
    meta, refs = refs[0], refs[1:]
    stored, refs = refs[:seq_size], refs[seq_size:]
    weights, refs = refs[: 2 * count], refs[2 * count :]
    pieces, refs = refs[:arrays], refs[arrays:]
    pieces = [pieces[at].at[index] for at, index in places]
    prior, refs = (refs[0], refs[1:]) if has_prior else (None, refs)
    table, refs = (None, refs) if finds else (refs[0], refs[1:])
    levels = seq_size.bit_length()
    outs, refs = refs[:levels], refs[levels:]
    grads, refs = (refs[:2], refs[2:]) if last else (refs[:1], refs[1:])
    if finds:
        table, refs = refs[0], refs[1:]
    pair, kv, d_kv, found, sem = refs
    block = stored[0].shape[0]
    rows = d_kv.shape[0]
    tokens = spans * SPAN
    scale = HEAD_SIZE ** (-0.5)
    keys_first = meta[2] == 1
    if finds:
        for k, rows_of in enumerate(relative_positions(pieces[:seq_size], meta[0], per_owner, tokens)):
            table[8 * k : 8 * k + 8, :] = rows_of
    copy = pltpu.make_async_copy(table, found, sem)
    copy.start()
    for i in range(count):
        first, second = weights[2 * i][...], weights[2 * i + 1][...]
        pair[:, 2 * i * HEAD_SIZE : (2 * i + 1) * HEAD_SIZE] = jnp.where(keys_first, first, second)
        pair[:, (2 * i + 1) * HEAD_SIZE : (2 * i + 2) * HEAD_SIZE] = jnp.where(keys_first, second, first)
        wide = slice(2 * i * HEAD_SIZE, 2 * (i + 1) * HEAD_SIZE)
        for n in range(seq_size):
            kv[n * block : (n + 1) * block, wide] = jnp.dot(
                stored[n][...], pair[:, wide], preferred_element_type=jnp.float32
            ).astype(jnp.bfloat16)
    d_kv[...] = jnp.zeros_like(d_kv)
    copy.wait()
    units = [(i, *spot) for i in range(count) for spot in spots_of(found, seq_size, spans)]
    reads, queries, grad_rows, scores, d_probs = [], [], [], [], []
    for i, k, c, starts in units:
        wide = slice(2 * i * HEAD_SIZE, 2 * (i + 1) * HEAD_SIZE)
        source, at = takes[i]
        taken = slice(at * HEAD_SIZE, (at + 1) * HEAD_SIZE)
        read = jnp.concatenate([kv[pl.ds(start, NLEN), wide] for start in starts], axis=0)
        query = pieces[source * seq_size + k][c * SPAN : (c + 1) * SPAN, taken]
        grad = pieces[source * seq_size + k][tokens + c * SPAN : tokens + (c + 1) * SPAN, taken]
        reads.append((read[:, :HEAD_SIZE], read[:, HEAD_SIZE:]))
        queries.append(query)
        grad_rows.append(grad)
        scores.append(lax.dot_general(query, reads[-1][0], NT, preferred_element_type=jnp.float32))
        d_probs.append(lax.dot_general(grad, reads[-1][1], NT, preferred_element_type=jnp.float32))
    probs_low, d_scores = [], []
    for score, d_prob in zip(scores, d_probs):
        expos = jnp.exp(score * scale)
        probs = expos * (1.0 / jnp.sum(expos, axis=-1, keepdims=True))
        delta = jnp.sum(probs * d_prob, axis=-1, keepdims=True)
        probs_low.append(probs.astype(jnp.bfloat16))
        d_scores.append((probs * (d_prob - delta) * scale).astype(jnp.bfloat16))
    for n, (i, k, c, _) in enumerate(units):
        keys, values = reads[n]
        span = slice(c * SPAN, (c + 1) * SPAN)
        columns = slice(i * HEAD_SIZE, (i + 1) * HEAD_SIZE)
        item_of(outs, k)[0, span, columns] = jnp.dot(
            probs_low[n], values, preferred_element_type=jnp.float32
        ).astype(jnp.bfloat16)
        item_of(outs, k)[1, span, columns] = jnp.dot(
            d_scores[n], keys, preferred_element_type=jnp.float32
        ).astype(jnp.bfloat16)
    both = [
        (
            lax.dot_general(d_scores[n], queries[n], TN, preferred_element_type=jnp.float32),
            lax.dot_general(probs_low[n], grad_rows[n], TN, preferred_element_type=jnp.float32),
        )
        for n in range(len(units))
    ]
    for n, (i, _, _, starts) in enumerate(units):
        for r, start in enumerate(starts):
            for part in range(2):
                wide = slice((2 * i + part) * HEAD_SIZE, (2 * i + part + 1) * HEAD_SIZE)
                d_kv[pl.ds(start, NLEN), wide] += both[n][part][r * NLEN : (r + 1) * NLEN]
    half = rows // 2
    for part in range(2):
        place = slice(part * half, (part + 1) * half)
        term = lax.dot_general(
            d_kv[place, :].astype(jnp.bfloat16), pair[...], NT, preferred_element_type=jnp.float32
        )
        if has_prior:
            term = term + prior[place, :].astype(jnp.float32)
        if last:
            grads[part][...] = term.astype(grads[part].dtype)
        else:
            grads[0][place, :] = term.astype(grads[0].dtype)


def attention(meta, table, stored, weights, takes, spans, per_owner, prior, last):
    seq_size = len(stored)
    sources = []
    for source, _ in takes:
        if not any(source is known for known in sources):
            sources.append(source)
    takes = [([source is known for known in sources].index(True), at) for source, at in takes]
    arrays, places = operands_of([item for source in sources for item in source])
    block, width = stored[0].shape
    rows = seq_size * block
    count = len(weights) // 2
    prior = [] if prior is None else [prior]
    vmem = pl.BlockSpec(memory_space=pltpu.VMEM)
    finds = table is None
    operands = [*stored, *weights, *arrays, *prior] + ([] if finds else [table])
    table_shape = (8 * seq_size, HEAD_SIZE)
    out_shape = bundles(seq_size, (2, spans * SPAN, count * HEAD_SIZE), jnp.bfloat16)
    levels = len(out_shape)
    if last:
        out_shape.append(jax.ShapeDtypeStruct((rows // 2, width), jnp.float32))
        out_shape.append(jax.ShapeDtypeStruct((rows // 2, width), jnp.bfloat16))
    else:
        out_shape.append(jax.ShapeDtypeStruct((rows, width), jnp.bfloat16))
    grads = len(out_shape) - levels
    scratch = [
        pltpu.VMEM((width, 2 * count * HEAD_SIZE), jnp.bfloat16),
        pltpu.VMEM((rows, 2 * count * HEAD_SIZE), jnp.bfloat16),
        pltpu.VMEM((rows, 2 * count * HEAD_SIZE), jnp.float32),
        pltpu.SMEM(table_shape, jnp.int32),
        pltpu.SemaphoreType.DMA,
    ]
    if finds:
        out_shape.append(jax.ShapeDtypeStruct(table_shape, jnp.int32))
    outs = pl.pallas_call(
        functools.partial(
            attention_body, seq_size, spans, takes, places, len(arrays), per_owner, finds, len(prior), last
        ),
        out_shape=out_shape,
        in_specs=[pl.BlockSpec(memory_space=pltpu.SMEM)] + [vmem] * len(operands),
        out_specs=[vmem] * len(out_shape),
        scratch_shapes=scratch,
        compiler_params=pltpu.CompilerParams(vmem_limit_bytes=vmem_bytes(rows)),
        cost_estimate=pl.CostEstimate(
            flops=int(2.4e9) if last and len(prior) else 0, bytes_accessed=0, transcendentals=0
        ),
        name="attention",
    )(meta, *operands)
    return outs[:levels], outs[levels : levels + grads], outs[-1] if finds else table


def unpack_body(seq_size, groups, places, meta, *refs):
    attended, grad_queries = refs[-2:]
    own, first = meta[0], meta[1]
    for g, heads in enumerate(groups):
        for k in range(seq_size):
            at, index = places[g * seq_size + k]
            for i, r in enumerate(heads):
                column = pl.multiple_of(((first ^ r) * seq_size + (own ^ k)) * HEAD_SIZE, HEAD_SIZE)
                place = slice(i * HEAD_SIZE, (i + 1) * HEAD_SIZE)
                attended[0, :, pl.ds(column, HEAD_SIZE)] = refs[at][index, 0, :, place]
                grad_queries[0, :, pl.ds(column, HEAD_SIZE)] = refs[at][index, 1, :, place]


def unpack(meta, items, groups, seq_size):
    arrays, places = operands_of(items)
    tokens = arrays[0].shape[2]
    shape = jax.ShapeDtypeStruct((1, tokens, HEADS * HEAD_SIZE), jnp.bfloat16)
    vmem = pl.BlockSpec(memory_space=pltpu.VMEM)
    return pl.pallas_call(
        functools.partial(unpack_body, seq_size, groups, places),
        out_shape=[shape, shape],
        in_specs=[pl.BlockSpec(memory_space=pltpu.SMEM)] + [vmem] * len(arrays),
        out_specs=[vmem, vmem],
        compiler_params=pltpu.CompilerParams(vmem_limit_bytes=SMALL_BYTES),
        cost_estimate=pl.CostEstimate(flops=0, bytes_accessed=0, transcendentals=0),
        name="unpack",
    )(meta, *arrays)


def weight_slice(kv_weight, column):
    return lax.dynamic_slice_in_dim(kv_weight, column, HEAD_SIZE, axis=1)


def whole_weights(kv_weight, own, seq_size):
    whole = lax.all_gather(kv_weight, "dp", axis=1, tiled=True)
    pairs = []
    for r in range(HEADS // seq_size):
        column = (r * seq_size + own) * HEAD_SIZE
        pairs.append((weight_slice(whole, column), weight_slice(whole, column + HEADS * HEAD_SIZE)))
    return pairs


def tie(*values):
    return lax.optimization_barrier(values)


def fold(total, arrived):
    total = total + arrived.astype(jnp.float32)
    half = total.shape[0] // 2
    return total[:half], total[half:].astype(jnp.bfloat16)


def tie_items(value, items):
    tied = lax.optimization_barrier((value, [array for array, _ in items]))
    return tied[0], [(array, index) for array, (_, index) in zip(tied[1], items)]


def per_device(dp_size, seq_size, queries, grad_out, encoded, kv_weight, neighbour_ids, slot_map):
    own = lax.axis_index("seq")
    place = lax.axis_index("dp")
    bits = seq_size.bit_length() - 1
    per_owner = encoded.shape[1]
    spans = neighbour_ids.shape[1]
    tokens = queries.shape[1]
    width = encoded.shape[3]
    pool_size = slot_map.shape[1]
    assert pool_size <= 256 and 1 << bits == seq_size and per_owner & (per_owner - 1) == 0
    split = dp_size == 8 and 2 * HEADS == dp_size * seq_size
    send = functools.partial(xor_send, axis="seq", size=seq_size)
    move = functools.partial(xor_send, axis="dp", size=dp_size)

    if split:
        first = place % (HEADS // seq_size)
        keys_first = (place < dp_size // 2).astype(jnp.int32)
        groups = [(0,), (1, 2), (3,)]
        packed = [(0,), (1, 2, 3)]
    else:
        first, keys_first = place * 0, place * 0 + 1
        groups = packed = [tuple(range(HEADS // seq_size))]

    head_meta = jnp.stack([own, first, keys_first, place])
    pieces = pack(head_meta, neighbour_ids, slot_map, queries, grad_out, packed, seq_size)
    stored = [encoded[0].reshape(per_owner * NLEN, width)]
    if not split:
        for level in range(bits - 1, -1, -1):
            stored = stored + [send(rows, bit=1 << level) for rows in stored]
    if split:
        mine = weight_slice(kv_weight, own * HEAD_SIZE)
        stored = stored + [send(stored[0], bit=2)]
        stored = stored + [send(rows, bit=1) for rows in stored]
        early = cross(pieces[0], seq_size, bits)
        far, near, side, late = tie(move(mine, bit=4), move(mine, bit=2), move(mine, bit=1), pieces[1])
        near_far = move(far, bit=2)
        side_far = move(far, bit=1)
        early = forward(early, seq_size)
        late = cross(late, seq_size, bits)
        attend = functools.partial(attention, head_meta, spans=spans, per_owner=per_owner)
        outs, (grads,), table = attend(
            None, stored, [mine, far], [(early, 0)], prior=None, last=False
        )
        near_far, outs = tie(near_far, outs)
        parts_a = cross(outs, seq_size, bits)
        near_far, side_far, side, near, late, grads = tie(near_far, side_far, side, near, late, grads)
        side_near_far, side_near = move(near_far, bit=1), move(side, bit=2)
        late = forward(late, seq_size)
        outs, (grads,), _ = attend(
            table, stored, [side, side_far, near, near_far], [(late, 0), (late, 1)], prior=grads, last=False
        )
        parts_b = cross(outs, seq_size, bits)
        grads, parts_a = tie(grads, parts_a)
        outs, grads, _ = attend(
            table, stored, [side_near, side_near_far], [(late, 2)], prior=grads, last=True
        )
        parts_c = cross(outs, seq_size, bits)
        grads, parts_b = tie(grads, parts_b)
        total, leaving = fold(grads[0], send(grads[1], bit=1))
        items = [item for parts in (parts_a, parts_b, parts_c) for item in forward(parts, seq_size)]
    else:
        weights = [block for pair in whole_weights(kv_weight, own, seq_size) for block in pair]
        early = exchange(pieces[0], seq_size)
        takes = [(early, i) for i in range(HEADS // seq_size)]
        outs, grads, _ = attention(head_meta, None, stored, weights, takes, spans, per_owner, None, True)
        items = exchange(outs, seq_size)
    if not split:
        total, leaving = grads
        for level in range(bits - 1):
            total, leaving = fold(total, send(leaving, bit=1 << level))
    total = total + send(leaving, bit=1 << (bits - 1)).astype(jnp.float32)
    attended, grad_queries = unpack(head_meta, items, groups, seq_size)
    return attended, grad_queries, total.reshape(1, per_owner, NLEN, width)


def solution(mesh):
    in_specs = (
        P("dp", "seq", None),
        P("dp", "seq", None),
        P("dp", "seq", None, None),
        P(None, "dp"),
        P("dp", "seq", None),
        P("dp", None),
    )
    out_specs = (P("dp", "seq", None), P("dp", "seq", None), P("dp", "seq", None, None))
    return jax.shard_map(
        functools.partial(per_device, mesh.shape["dp"], mesh.shape["seq"]),
        mesh=mesh,
        in_specs=in_specs,
        out_specs=out_specs,
        check_vma=False,
    )
```
